512 devices in a mesh: wide: 64 (over z, x, core), grp: 8 (over y).
Axes of the slice: x: 4, y: 8, z: 8, core: 2. Of those that a mesh axis runs over, the one named last changes fastest.
Arguments:
- amplitudes: float32 [256, 128, 128], P('wide'), may hold values from -6 to 6
- integrals: float32 [256, 128, 128], P('wide'), may hold values from -0.046875 to 0.046875
- residual_in: float32 [256, 128, 128], P('wide'), may hold values from -6 to 6
- task_lists: int32 [64, 8, 128, 3], P('wide', 'grp'), may hold values from 0 to 63
- task_counts: int32 [64, 8], P('wide'), may hold values from 1 to 128, 576 in all within a row
- amp_wanted: int32 [64, 64], P('wide'), may hold values from 0 to 3
- int_wanted: int32 [64, 64], P('wide'), may hold values from 0 to 3
- res_targets: int32 [64, 64], P('wide'), may hold values from 0 to 3
Outputs:
- residual_out: float32 [256, 128, 128], P('wide')
The draws below stay inside these ranges and needn't reach their ends.
Inputs may be any that keep to these rules, and one draw needn't show every extreme that they name: `task_counts`: the counts of one group's 8 members add up to 576; in every group one member has exactly 128.
All inputs are finite; a program needn't handle non-finite values.
Results may differ from the reference program's by a relative error of at most 0.0003.
Values sent between devices are 32-bit elements; how exact they have to be, the bound alone decides.
No kernel may reach another device: no remote copies, remote signals or barrier semaphores. Data moves between devices by JAX's collectives and lax.ppermute only.
A program may use at most 64 MiB of HBM per device.

```python
import math
import jax
import jax.numpy as jnp
import numpy as np
from jax import lax

TB = 128
TILES_DEV = 4
TPD = 128
NTILES = 256
GROUP_TASKS = 576
N_WIDE = 64
N_GRP = 8


def with_ends(array, own_key, smallest, high):
    dims = array.shape
    place = [jax.random.randint(jax.random.fold_in(own_key, axis), (), 0, dims[axis]) for axis in range(len(dims))]
    array = array.at[tuple(place)].set(smallest)
    longest = dims.index(max(dims))
    place[longest] = (place[longest] + 1) % dims[longest]
    return array.at[tuple(place)].set(high)


def block_levels(key, extent, pieces, low, high):
    loudness, own = 1.0, jax.random.fold_in(key, 6)
    for position, shards_of in pieces:
        draws = jnp.exp(jax.random.uniform(jax.random.fold_in(own, position), (shards_of,), jnp.float32, low / len(pieces), high / len(pieces)))
        loudness = loudness * jnp.repeat(draws, extent[position] // shards_of).reshape([-1 if axis == position else 1 for axis in range(len(extent))])
    return loudness


def profile(number_of, total, most, lean):
    weights = [(1 << 20) // math.isqrt(grade ** lean) + 1 for grade in range(2, number_of + 1)]
    spare, holding = total - most - (number_of - 1), [1] * (number_of - 1)
    while spare > 0:
        candidates = [i for i in range(number_of - 1) if holding[i] < most]
        mass, budget = sum([weights[i] for i in candidates]), spare
        for i in candidates:
            more = min(most - holding[i], max(1, budget * weights[i] // mass), spare)
            holding[i] = holding[i] + more
            spare = spare - more
    return np.array([most] + holding)


def uneven_parts(rng, amount, total, reach, lean):
    if amount == 2:
        one = jax.random.randint(rng, (), max(1, total - reach), min(reach, total - 1) + 1)
        return jnp.stack([one, total - one])
    lengths = jnp.asarray(profile(amount, total, reach, lean), jnp.int32)
    twos = (amount - 1) // 2
    donor, taker = lengths[1:1 + 2 * twos:2], lengths[2:2 + 2 * twos:2]
    room = jnp.minimum(donor - 1, reach - taker)
    shifted = jax.random.randint(jax.random.fold_in(rng, 1), (twos,), 0, 1 << 20) % (room + 1)
    lengths = lengths.at[1:1 + 2 * twos:2].set(donor - shifted).at[2:2 + 2 * twos:2].set(taker + shifted)
    return lengths[jax.random.permutation(jax.random.fold_in(rng, 2), amount)]


def normal_values(own_key, extent, scale, limit, shards=(), kind=jnp.bfloat16):
    values = scale * jax.random.normal(own_key, extent, jnp.float32)
    if shards:
        values = values * block_levels(own_key, extent, shards, -0.22, 0.18)
    return jnp.clip(values, -limit, limit).astype(kind)


def setup_inputs(seed: int = 0) -> dict:
    key_of = jax.random.split(jax.random.key(seed), 9)
    amplitudes = normal_values(key_of[0], (NTILES, TB, TB), 1.0, 6.0, ((0, 64),), jnp.float32)
    integrals = normal_values(key_of[1], (NTILES, TB, TB), (TB * GROUP_TASKS // TILES_DEV) ** -0.5, 0.046875, ((0, 64),), jnp.float32)
    residual_in = normal_values(key_of[2], (NTILES, TB, TB), 1.0, 6.0, ((0, 64),), jnp.float32)
    task_lists = with_ends(jax.random.randint(key_of[3], (N_WIDE, N_GRP, TPD, 3), 0, N_WIDE), jax.random.fold_in(key_of[3], 1), 0, N_WIDE - 1).astype(jnp.int32)
    task_counts = jax.vmap(lambda own: uneven_parts(own, N_GRP, GROUP_TASKS, TPD, 2))(jax.random.split(key_of[4], N_WIDE)).reshape((N_WIDE, N_GRP)).astype(jnp.int32)
    amp_wanted = with_ends(jax.random.randint(key_of[5], (N_WIDE, N_WIDE), 0, TILES_DEV), jax.random.fold_in(key_of[5], 1), 0, TILES_DEV - 1).astype(jnp.int32)
    int_wanted = with_ends(jax.random.randint(key_of[6], (N_WIDE, N_WIDE), 0, TILES_DEV), jax.random.fold_in(key_of[6], 1), 0, TILES_DEV - 1).astype(jnp.int32)
    res_targets = with_ends(jax.random.randint(key_of[7], (N_WIDE, N_WIDE), 0, TILES_DEV), jax.random.fold_in(key_of[7], 1), 0, TILES_DEV - 1).astype(jnp.int32)
    return dict(amplitudes=amplitudes, integrals=integrals, residual_in=residual_in, task_lists=task_lists, task_counts=task_counts, amp_wanted=amp_wanted, int_wanted=int_wanted, res_targets=res_targets)


def reference(amplitudes, integrals, residual_in, task_lists, task_counts, amp_wanted, int_wanted, res_targets):
    owners = jnp.arange(N_WIDE, dtype=jnp.int32)
    slot_ids = jnp.arange(TPD, dtype=jnp.int32)

    def one_group(result, group_id):
        tiles_a = amplitudes[owners * TILES_DEV + amp_wanted[group_id]]
        tiles_b = integrals[owners * TILES_DEV + int_wanted[group_id]]
        live_slots = (slot_ids[None, :] < task_counts[group_id][:, None]).astype(jnp.float32)

        def one_member(running, member_item):
            member_tasks, member_live = member_item
            left = tiles_a[member_tasks[:, 0]]
            right = tiles_b[member_tasks[:, 1]]
            products = jnp.einsum("kab,kcb->kac", left, right, precision=lax.Precision.HIGHEST,
                                  preferred_element_type=jnp.float32)
            products = products * member_live[:, None, None]
            return running.at[member_tasks[:, 2]].add(products), None

        start_acc = jnp.zeros((N_WIDE, TB, TB), jnp.float32)
        partial_value, _ = lax.scan(one_member, start_acc, (task_lists[group_id], live_slots))
        result = result.at[owners * TILES_DEV + res_targets[group_id]].add(partial_value)
        return result, None

    residual_out, _ = lax.scan(one_group, residual_in, owners)
    return residual_out
```

```python
import jax
import jax.numpy as jnp
from jax import lax
from jax.experimental import pallas as pl
from jax.experimental.pallas import tpu as pltpu
from jax.sharding import Mesh, PartitionSpec as P

TB = 128
TILES = 4
OWNERS = 64
MEMBERS = 8
KS = TB // MEMBERS
ALL_TILES = OWNERS * TILES
ROWS = 2 * TILES * KS + 3 * MEMBERS
A_AT, B_AT, T_AT = 0, TILES * KS, 2 * TILES * KS
LISTS = OWNERS * MEMBERS
CHUNK = 256
SUB = 32

NT = (((1,), (1,)), ((), ()))
TN = (((0,), (0,)), ((), ()))


def dot(a, b, dims=(((1,), (0,)), ((), ()))):
    return lax.dot_general(a, b, dims, preferred_element_type=jnp.float32)


def task_kernel(tasks_ref, counts_ref, amp_ref, int_ref, res_ref, out_ref):
    live = counts_ref[0, lax.axis_index("grp")]
    slot = lax.broadcasted_iota(jnp.int32, (TB, OWNERS), 0)
    owner = lax.broadcasted_iota(jnp.int32, (TB, OWNERS), 1)
    number = lax.broadcasted_iota(jnp.int32, (8, OWNERS), 1) * TILES
    rows = []
    for column, table in enumerate((amp_ref, int_ref, res_ref)):
        hit = tasks_ref[:, column : column + 1] == owner
        if column == 2:
            hit = hit & (slot < live)
        names = number + table[0:1, :] + (1 if column == 2 else 0)
        rows.append(dot(names.astype(jnp.bfloat16), hit.astype(jnp.bfloat16), NT)[0:1])
    rows[2] = rows[2] - 1.0
    block = jnp.concatenate(rows + [jnp.zeros((5, TB), jnp.float32)], axis=0)
    for member in range(MEMBERS):
        out_ref[member] = block


def payload_kernel(amp_ref, int_ref, tasks_ref, out_ref, turned):
    first = pl.multiple_of(lax.axis_index("grp") * KS, KS)
    for at, tiles in ((A_AT, amp_ref), (B_AT, int_ref)):
        for t in range(TILES):
            turned[...] = tiles[t].T
            rows = turned[pl.ds(first, KS), :]
            for z in range(8):
                out_ref[z, at + t * KS : at + (t + 1) * KS, :] = rows
    for kind in range(3):
        rows = jnp.concatenate([tasks_ref[m, kind : kind + 1, :] for m in range(MEMBERS)], axis=0)
        for z in range(8):
            out_ref[z, T_AT + kind * MEMBERS : T_AT + (kind + 1) * MEMBERS, :] = rows


def ladder_kernel(own_ref, other_ref, out_ref, sa, sb, lhs, rhs, acc, wanted, names, lists_v, lists_s, sem):
    me = ((lax.axis_index("z") * 4) + lax.axis_index("x")) * 2 + lax.axis_index("core")
    core = lax.axis_index("core")

    def spread(index, _):
        x, z = index // 8, index % 8
        for side, ref, c in ((0, own_ref, core), (1, other_ref, 1 - core)):
            owner = (z * 4 + x) * 2 + c
            to = pl.ds(pl.multiple_of(owner * TILES * KS, TILES * KS), TILES * KS)
            for at, store in ((A_AT, sa), (B_AT, sb)):
                value = ref[x, z, at : at + TILES * KS, :]
                high = value.astype(jnp.bfloat16)
                store[to, 0:TB] = high
                store[to, TB : 2 * TB] = (value - high.astype(jnp.float32)).astype(jnp.bfloat16)
        return 0

    lax.fori_loop(0, 32, spread, 0)
    sa[ALL_TILES * KS :, :] = jnp.zeros((KS, 2 * TB), jnp.bfloat16)
    acc[...] = jnp.zeros_like(acc)

    for side, ref in enumerate((own_ref, other_ref)):
        for x in range(4):
            for z in range(0, 8, 2):
                at = (side * 32 + x * 8 + z) * MEMBERS
                for kind in range(3):
                    rows = [ref[x, z + i, T_AT + kind * MEMBERS : T_AT + (kind + 1) * MEMBERS, :] for i in range(2)]
                    rows = jnp.concatenate(rows, axis=0)
                    if kind == 2:
                        wanted[at : at + 2 * MEMBERS, :] = rows
                    else:
                        names[at : at + 2 * MEMBERS, kind * TB : (kind + 1) * TB] = rows.astype(jnp.bfloat16)

    upto = lax.broadcasted_iota(jnp.int32, (TB, TB), 0) <= lax.broadcasted_iota(jnp.int32, (TB, TB), 1)
    upto = upto.astype(jnp.bfloat16)
    ones = jnp.ones((8, TB), jnp.bfloat16)

    def one_round(state):
        turn, _ = state
        base = turn * CHUNK
        for t in range(TILES):
            hit = wanted[...] == (me * TILES + t).astype(jnp.float32)
            hit_f = hit.astype(jnp.float32)
            hit_b = hit_f.astype(jnp.bfloat16)
            place = dot(hit_b, upto)
            names[:, 2 * TB :] = (place * hit_f).astype(jnp.bfloat16)
            totals = dot(ones, hit_b, NT)
            carry = jnp.zeros((8, 1), jnp.float32)
            upper = []
            for i in range(LISTS // TB):
                piece = totals[:, i * TB : (i + 1) * TB]
                upper.append(dot(piece.astype(jnp.bfloat16), upto) + carry)
                carry = carry + jnp.sum(piece, axis=1, keepdims=True)
            upper = jnp.concatenate(upper, axis=1)
            lower = upper - totals
            rank = (base + lax.broadcasted_iota(jnp.int32, (CHUNK, LISTS), 0)).astype(jnp.float32)
            row = (lower[0:1] <= rank) & (rank < upper[0:1])
            before = jnp.sum(jnp.where(row, lower[0:1], 0.0), axis=1, keepdims=True)
            found = dot(row.astype(jnp.float32).astype(jnp.bfloat16), names[...])
            pick = found[:, 2 * TB :] == rank[:, 0:1] + 1.0 - before
            left = dot(ones, jnp.where(pick, found[:, 0:TB], 0.0).astype(jnp.bfloat16), NT)
            right = dot(ones, jnp.where(pick, found[:, TB : 2 * TB], 0.0).astype(jnp.bfloat16), NT)
            entry = (base + lax.broadcasted_iota(jnp.int32, (8, CHUNK), 1)).astype(jnp.float32)
            code = jnp.where(entry < carry, left * 256.0 + right, float(ALL_TILES * 256))
            lists_v[t : t + 1, :] = code[0:1].astype(jnp.int32)
            lists_v[TILES + t : TILES + t + 1, :] = jnp.broadcast_to(carry[0:1], (1, CHUNK)).astype(jnp.int32)
        copy = pltpu.make_async_copy(lists_v, lists_s, sem)
        copy.start()
        copy.wait()
        most = jnp.int32(0)
        for t in range(TILES):
            total = lists_s[TILES + t, 0]
            most = jnp.maximum(most, total)
            here = jnp.clip(total - base, 0, CHUNK)

            def block(index, _, t=t):
                for i in range(SUB):
                    code = lists_s[t, index * SUB + i]
                    a = pl.multiple_of((code >> 8) * KS, KS)
                    b = pl.multiple_of((code & 255) * KS, KS)
                    lhs[i * KS : (i + 1) * KS, :] = sa[pl.ds(a, KS), :]
                    rhs[i * KS : (i + 1) * KS, :] = sb[pl.ds(b, KS), :]
                acc[t] += dot(lhs[...], rhs[...], TN)
                return 0

            lax.fori_loop(0, (here + SUB - 1) // SUB, block, 0)
        return turn + 1, (most + CHUNK - 1) // CHUNK

    lax.while_loop(lambda s: s[0] < s[1], one_round, (jnp.int32(0), jnp.int32(1)))
    for t in range(TILES):
        total = (acc[t, 0:TB, 0:TB] + acc[t, 0:TB, TB:]) + (acc[t, TB:, 0:TB] + acc[t, TB:, TB:])
        for m in range(MEMBERS):
            out_ref[m, t] = total[m * KS : (m + 1) * KS, :]


VMEM = pl.BlockSpec(memory_space=pltpu.VMEM)
SMEM = pl.BlockSpec(memory_space=pltpu.SMEM)
PARAMS = pltpu.CompilerParams(vmem_limit_bytes=48 * 1024 * 1024)


def swap(block, axis):
    return lax.all_to_all(block, axis, split_axis=0, concat_axis=0, tiled=True)


def local(amplitudes, integrals, residual_in, task_lists, task_counts, amp_wanted, int_wanted, res_targets):
    f32 = jnp.float32
    tasks = pl.pallas_call(
        task_kernel,
        out_shape=jax.ShapeDtypeStruct((MEMBERS, 8, TB), f32),
        in_specs=[VMEM, SMEM, VMEM, VMEM, VMEM],
        out_specs=VMEM,
    )(task_lists[0, 0], task_counts, amp_wanted, int_wanted, res_targets)
    tasks = swap(tasks, "grp")
    payload = pl.pallas_call(
        payload_kernel,
        out_shape=jax.ShapeDtypeStruct((8, ROWS, TB), f32),
        in_specs=[VMEM] * 3,
        out_specs=VMEM,
        scratch_shapes=[pltpu.VMEM((TB, TB), f32)],
    )(amplitudes, integrals, tasks)
    along_z = swap(payload, "z")
    own = swap(jnp.broadcast_to(along_z[None], (4, 8, ROWS, TB)), "x")
    other = lax.ppermute(own, "core", [(0, 1), (1, 0)])
    bf16 = jnp.bfloat16
    partial = pl.pallas_call(
        ladder_kernel,
        out_shape=jax.ShapeDtypeStruct((MEMBERS, TILES, KS, TB), f32),
        in_specs=[VMEM, VMEM],
        out_specs=VMEM,
        scratch_shapes=[
            pltpu.VMEM(((ALL_TILES + 1) * KS, 2 * TB), bf16),
            pltpu.VMEM((ALL_TILES * KS, 2 * TB), bf16),
            pltpu.VMEM((SUB * KS, 2 * TB), bf16),
            pltpu.VMEM((SUB * KS, 2 * TB), bf16),
            pltpu.VMEM((TILES, 2 * TB, 2 * TB), f32),
            pltpu.VMEM((LISTS, TB), f32),
            pltpu.VMEM((LISTS, 3 * TB), bf16),
            pltpu.VMEM((2 * TILES, CHUNK), jnp.int32),
            pltpu.SMEM((2 * TILES, CHUNK), jnp.int32),
            pltpu.SemaphoreType.DMA,
        ],
        compiler_params=PARAMS,
    )(own, other)
    member = lax.axis_index("grp")
    rows = lax.dynamic_slice_in_dim(residual_in, member * KS, KS, 1)
    rows = rows + jnp.sum(swap(partial, "grp"), axis=0)
    whole = swap(jnp.broadcast_to(rows[None], (MEMBERS, TILES, KS, TB)), "grp")
    return whole.transpose(1, 0, 2, 3).reshape(TILES, TB, TB)


def solution(mesh):
    fine = Mesh(mesh.devices.reshape(8, 4, 2, MEMBERS), ("z", "x", "core", "grp"))
    wide = ("z", "x", "core")
    placed = (
        P(wide, None, None),
        P(wide, None, None),
        P(wide, None, None),
        P(wide, "grp", None, None),
        P(wide, None),
        P(wide, None),
        P(wide, None),
        P(wide, None),
    )
    return jax.shard_map(local, mesh=fine, in_specs=placed, out_specs=P(wide, None, None), check_vma=False)
```

```python
import jax
import jax.numpy as jnp
from jax import lax
from jax.experimental import pallas as pl
from jax.experimental.pallas import tpu as pltpu
from jax.sharding import Mesh, PartitionSpec as P

TB = 128
TILES = 4
OWNERS = 64
MEMBERS = 8
KS = TB // MEMBERS
ALL_TILES = OWNERS * TILES
ROWS = 2 * TILES * KS + 3 * MEMBERS
A_AT, B_AT, T_AT = 0, TILES * KS, 2 * TILES * KS
LISTS = OWNERS * MEMBERS
CHUNK = 256
SUB = 32

NT = (((1,), (1,)), ((), ()))
TN = (((0,), (0,)), ((), ()))


def dot(a, b, dims=(((1,), (0,)), ((), ()))):
    return lax.dot_general(a, b, dims, preferred_element_type=jnp.float32)


def task_kernel(tasks_ref, counts_ref, amp_ref, int_ref, res_ref, out_ref):
    live = counts_ref[0, lax.axis_index("grp")]
    owner = lax.broadcasted_iota(jnp.int32, (OWNERS, TB), 0)
    slot = lax.broadcasted_iota(jnp.int32, (OWNERS, TB), 1)
    number = lax.broadcasted_iota(jnp.int32, (8, OWNERS), 1) * TILES
    for kind, table in enumerate((amp_ref, int_ref, res_ref)):
        hit = tasks_ref[0, kind] == owner
        if kind == 2:
            hit = hit & (slot < live)
        names = number + table[0:1, :] + (1 if kind == 2 else 0)
        row = dot(names.astype(jnp.bfloat16), hit.astype(jnp.bfloat16))[0:1]
        row = row - 1.0 if kind == 2 else row
        for m in range(MEMBERS):
            out_ref[m, kind : kind + 1, :] = row


def turn_kernel(amp_ref, int_ref, out_ref, turned):
    first = pl.multiple_of(lax.axis_index("grp") * KS, KS)
    for at, tiles in ((A_AT, amp_ref), (B_AT, int_ref)):
        for t in range(TILES):
            turned[t] = tiles[t].T
        for t in range(TILES):
            out_ref[at + t * KS : at + (t + 1) * KS, :] = turned[t, pl.ds(first, KS), :]


def payload_kernel(tiles_ref, lists_ref, out_ref):
    for kind in range(3):
        rows = jnp.concatenate([lists_ref[m, kind : kind + 1, :] for m in range(MEMBERS)], axis=0)
        for z in range(8):
            out_ref[z, T_AT + kind * MEMBERS : T_AT + (kind + 1) * MEMBERS, :] = rows
    for z in range(8):
        out_ref[z, 0:T_AT, :] = tiles_ref[...]


def ladder_kernel(*refs):
    out_ref, sa, sb, lhs, rhs, acc, wanted, names, lists_v, lists_s, sem = refs[10:]
    my_x = lax.axis_index("x")
    blocks = [(ref, side, *(((0, 0, 8), (3, 0, 8), (1, 0, 8), (2, 0, 4), (2, 4, 4))[i])) for side in range(2) for i, ref in enumerate(refs[side * 5 : side * 5 + 5])]
    me = ((lax.axis_index("z") * 4) + lax.axis_index("x")) * 2 + lax.axis_index("core")
    core = lax.axis_index("core")

    at = 0
    for ref, _, _, _, size in blocks:
        for z in range(0, size, 2):
            for kind in range(3):
                rows = [ref[z + i, T_AT + kind * MEMBERS : T_AT + (kind + 1) * MEMBERS, :] for i in range(2)]
                rows = jnp.concatenate(rows, axis=0)
                if kind == 2:
                    wanted[at : at + 2 * MEMBERS, :] = rows
                else:
                    names[at : at + 2 * MEMBERS, kind * TB : (kind + 1) * TB] = rows.astype(jnp.bfloat16)
            at += 2 * MEMBERS

    upto = lax.broadcasted_iota(jnp.int32, (TB, TB), 0) <= lax.broadcasted_iota(jnp.int32, (TB, TB), 1)
    upto = upto.astype(jnp.bfloat16)
    ones = jnp.ones((8, TB), jnp.bfloat16)

    def pick(base):
        hits = []
        for t in range(TILES):
            hit = wanted[...] == (me * TILES + t).astype(jnp.float32)
            hits.append(hit.astype(jnp.float32).astype(jnp.bfloat16))
        totals = [dot(ones, hit, NT) for hit in hits]
        for t in range(TILES):
            place = dot(hits[t], upto)
            names[:, (2 + t) * TB : (3 + t) * TB] = place.astype(jnp.bfloat16) * hits[t]
        lowers, uppers, sums = [], [], []
        for t in range(TILES):
            carry = jnp.zeros((8, 1), jnp.float32)
            upper = []
            pieces = [totals[t][:, i * TB : (i + 1) * TB] for i in range(LISTS // TB)]
            within = [dot(piece.astype(jnp.bfloat16), upto) for piece in pieces]
            for i in range(LISTS // TB):
                upper.append(within[i] + carry)
                carry = carry + within[i][:, TB - 1 : TB]
            uppers.append(jnp.concatenate(upper, axis=1))
            lowers.append(uppers[t] - totals[t])
            sums.append(carry)
        rank = (base + lax.broadcasted_iota(jnp.int32, (CHUNK, LISTS), 0)).astype(jnp.float32)
        entry = (base + lax.broadcasted_iota(jnp.int32, (8, CHUNK), 1)).astype(jnp.float32)
        rows = [(lowers[t][0:1] <= rank) & (rank < uppers[t][0:1]) for t in range(TILES)]
        before = [jnp.sum(jnp.where(rows[t], lowers[t][0:1], 0.0), axis=1, keepdims=True) for t in range(TILES)]
        rows = [row.astype(jnp.float32).astype(jnp.bfloat16) for row in rows]
        found = [dot(rows[t], names[:, 0 : 2 * TB]) for t in range(TILES)]
        places = [dot(rows[t], names[:, (2 + t) * TB : (3 + t) * TB]) for t in range(TILES)]
        for t in range(TILES):
            chosen = places[t] == rank[:, 0:1] + 1.0 - before[t]
            left = dot(ones, jnp.where(chosen, found[t][:, 0:TB], 0.0).astype(jnp.bfloat16), NT)
            right = dot(ones, jnp.where(chosen, found[t][:, TB : 2 * TB], 0.0).astype(jnp.bfloat16), NT)
            code = jnp.where(entry < sums[t], left * 256.0 + right, float(ALL_TILES * 256))
            lists_v[t : t + 1, :] = code[0:1].astype(jnp.int32)
            lists_v[TILES + t : TILES + t + 1, :] = jnp.broadcast_to(sums[t][0:1], (1, CHUNK)).astype(jnp.int32)

    def spread(index, _):
        for ref, side, step, first, size in blocks:
            if size == 4:
                ref = ref.at[pl.ds(index // 2, 1)]
            else:
                ref = ref.at[pl.ds(index, 1)]
            z = index // 2 + first if size == 4 else index
            c = core if side == 0 else 1 - core
            owner = (z * 4 + (my_x + step) % 4) * 2 + c
            to = pl.ds(pl.multiple_of(owner * TILES * KS, TILES * KS), TILES * KS)
            for at, store in ((A_AT, sa), (B_AT, sb)):
                value = ref[0, at : at + TILES * KS, :]
                high = value.astype(jnp.bfloat16)
                store[to, 0:TB] = high
                store[to, TB : 2 * TB] = (value - high.astype(jnp.float32)).astype(jnp.bfloat16)
        return 0

    def one_round(state):
        turn, _ = state
        base = turn * CHUNK
        pick(base)
        copy = pltpu.make_async_copy(lists_v, lists_s, sem)
        copy.start()

        @pl.when(turn == 0)
        def _():
            lax.fori_loop(0, 8, spread, 0)
            sa[ALL_TILES * KS :, :] = jnp.zeros((KS, 2 * TB), jnp.bfloat16)
            acc[...] = jnp.zeros_like(acc)

        copy.wait()
        most = lists_s[TILES, 0]
        for t in range(1, TILES):
            most = jnp.maximum(most, lists_s[TILES + t, 0])

        def block(index, _):
            for t in range(TILES):
                for i in range(SUB):
                    code = lists_s[t, index * SUB + i]
                    a = pl.multiple_of((code >> 8) * KS, KS)
                    b = pl.multiple_of((code & 255) * KS, KS)
                    lhs[t, i * KS : (i + 1) * KS, :] = sa[pl.ds(a, KS), :]
                    rhs[t, i * KS : (i + 1) * KS, :] = sb[pl.ds(b, KS), :]
            for t in range(TILES):
                acc[t] += dot(lhs[t], rhs[t], TN)
            return 0

        lax.fori_loop(0, (jnp.clip(most - base, 0, CHUNK) + SUB - 1) // SUB, block, 0)
        return turn + 1, (most + CHUNK - 1) // CHUNK

    lax.while_loop(lambda s: s[0] < s[1], one_round, (jnp.int32(0), jnp.int32(1)))
    for t in range(TILES):
        total = (acc[t, 0:TB, 0:TB] + acc[t, 0:TB, TB:]) + (acc[t, TB:, 0:TB] + acc[t, TB:, TB:])
        for m in range(MEMBERS):
            out_ref[m, t] = total[m * KS : (m + 1) * KS, :]


VMEM = pl.BlockSpec(memory_space=pltpu.VMEM)
SMEM = pl.BlockSpec(memory_space=pltpu.SMEM)
PARAMS = pltpu.CompilerParams(vmem_limit_bytes=48 * 1024 * 1024)


def shift(block, by):
    return lax.ppermute(block, "x", [(i, (i + by) % 4) for i in range(4)])


def swap(block, axis):
    return lax.all_to_all(block, axis, split_axis=0, concat_axis=0, tiled=True)


def local(amplitudes, integrals, residual_in, task_lists, task_counts, amp_wanted, int_wanted, res_targets):
    f32 = jnp.float32
    lists = pl.pallas_call(
        task_kernel,
        out_shape=jax.ShapeDtypeStruct((MEMBERS, 3, TB), f32),
        in_specs=[VMEM, SMEM, VMEM, VMEM, VMEM],
        out_specs=VMEM,
    )(task_lists.transpose(0, 3, 1, 2), task_counts, amp_wanted, int_wanted, res_targets)
    lists = swap(lists, "grp")
    tiles = pl.pallas_call(
        turn_kernel,
        out_shape=jax.ShapeDtypeStruct((T_AT, TB), f32),
        in_specs=[VMEM] * 2,
        out_specs=VMEM,
        scratch_shapes=[pltpu.VMEM((TILES, TB, TB), f32)],
    )(amplitudes, integrals)
    payload = pl.pallas_call(
        payload_kernel,
        out_shape=jax.ShapeDtypeStruct((8, ROWS, TB), f32),
        in_specs=[VMEM] * 2,
        out_specs=VMEM,
    )(tiles, lists)
    here = swap(payload, "z")
    left, right = shift(here, 1), shift(here, -1)
    near = [here, left, right, shift(left[:4], 1), shift(right[4:], -1)]
    far = [lax.ppermute(block, "core", [(0, 1), (1, 0)]) for block in near]
    bf16 = jnp.bfloat16
    partial = pl.pallas_call(
        ladder_kernel,
        out_shape=jax.ShapeDtypeStruct((MEMBERS, TILES, KS, TB), f32),
        in_specs=[VMEM] * 10,
        out_specs=VMEM,
        scratch_shapes=[
            pltpu.VMEM(((ALL_TILES + 1) * KS, 2 * TB), bf16),
            pltpu.VMEM((ALL_TILES * KS, 2 * TB), bf16),
            pltpu.VMEM((TILES, SUB * KS, 2 * TB), bf16),
            pltpu.VMEM((TILES, SUB * KS, 2 * TB), bf16),
            pltpu.VMEM((TILES, 2 * TB, 2 * TB), f32),
            pltpu.VMEM((LISTS, TB), f32),
            pltpu.VMEM((LISTS, (2 + TILES) * TB), bf16),
            pltpu.VMEM((2 * TILES, CHUNK), jnp.int32),
            pltpu.SMEM((2 * TILES, CHUNK), jnp.int32),
            pltpu.SemaphoreType.DMA,
        ],
        compiler_params=PARAMS,
    )(*near, *far)
    member = lax.axis_index("grp")
    rows = lax.dynamic_slice_in_dim(residual_in, member * KS, KS, 1)
    rows = rows + jnp.sum(swap(partial, "grp"), axis=0)
    whole = swap(jnp.broadcast_to(rows[None], (MEMBERS, TILES, KS, TB)), "grp")
    return whole.transpose(1, 0, 2, 3).reshape(TILES, TB, TB)


def solution(mesh):
    fine = Mesh(mesh.devices.reshape(8, 4, 2, MEMBERS), ("z", "x", "core", "grp"))
    wide = ("z", "x", "core")
    placed = (
        P(wide, None, None),
        P(wide, None, None),
        P(wide, None, None),
        P(wide, "grp", None, None),
        P(wide, None),
        P(wide, None),
        P(wide, None),
        P(wide, None),
    )
    return jax.shard_map(local, mesh=fine, in_specs=placed, out_specs=P(wide, None, None), check_vma=False)
```

```python
import jax
import jax.numpy as jnp
from jax import lax
from jax.experimental import pallas as pl
from jax.experimental.pallas import tpu as pltpu
from jax.sharding import Mesh, PartitionSpec as P

TB = 128
TILES = 4
OWNERS = 64
MEMBERS = 8
KS = TB // MEMBERS
ALL_TILES = OWNERS * TILES
ROWS = 2 * TILES * KS + 16
LIST_ROWS = 5
A_AT, B_AT, T_AT = 0, TILES * KS, 2 * TILES * KS
LISTS = OWNERS * LIST_ROWS
CHUNK = 256
SUB = 32
WAYS = 3
WIDTH = CHUNK + 128

NT = (((1,), (1,)), ((), ()))
TN = (((0,), (0,)), ((), ()))


def dot(a, b, dims=(((1,), (0,)), ((), ()))):
    return lax.dot_general(a, b, dims, preferred_element_type=jnp.float32)


def task_kernel(tasks_ref, counts_ref, amp_ref, int_ref, res_ref, out_ref):
    live = counts_ref[0, lax.axis_index("grp")]
    owner = lax.broadcasted_iota(jnp.int32, (OWNERS, TB), 0)
    slot = lax.broadcasted_iota(jnp.int32, (OWNERS, TB), 1)
    number = lax.broadcasted_iota(jnp.int32, (8, OWNERS), 1) * TILES
    for kind, table in enumerate((amp_ref, int_ref, res_ref)):
        hit = tasks_ref[0, kind] == owner
        if kind == 2:
            hit = hit & (slot < live)
        names = number + table[0:1, :] + (1 if kind == 2 else 0)
        row = dot(names.astype(jnp.bfloat16), hit.astype(jnp.bfloat16))[0:1]
        row = row - 1.0 if kind == 2 else row
        for m in range(MEMBERS):
            out_ref[m, kind : kind + 1, :] = row


def turn_kernel(amp_ref, int_ref, out_ref, turned):
    first = pl.multiple_of(lax.axis_index("grp") * KS, KS)
    for at, tiles in ((A_AT, amp_ref), (B_AT, int_ref)):
        for t in range(TILES):
            turned[t] = tiles[t].T
        for t in range(TILES):
            out_ref[at + t * KS : at + (t + 1) * KS, :] = turned[t, pl.ds(first, KS), :]


def payload_kernel(counts_ref, tiles_ref, lists_ref, out_ref, joined):
    joined[...] = jnp.full_like(joined, -1.0)
    lane = lax.broadcasted_iota(jnp.int32, (3, TB), 1)
    at = jnp.int32(0)
    for m in range(MEMBERS):
        row, by = at // TB, at % TB
        turned = pltpu.roll(lists_ref[m], by, 1)
        joined[row] = jnp.where(lane >= by, turned, joined[row])
        joined[row + 1] = jnp.where(lane < by, turned, joined[row + 1])
        at = at + counts_ref[0, m]
    rows = [joined[i, kind : kind + 1, :] for kind in range(3) for i in range(LIST_ROWS)]
    rows = jnp.concatenate(rows + [jnp.zeros((1, TB), jnp.float32)], axis=0)
    for z in range(8):
        out_ref[z, 0:T_AT, :] = tiles_ref[...]
        out_ref[z, T_AT:ROWS, :] = rows


def ladder_kernel(*refs):
    out_ref, sa, sb, acc, wanted, plain, names, lists_v, lists_s, sem = refs[10:]
    my_x = lax.axis_index("x")
    blocks = [(ref, side, *(((0, 0, 8), (3, 0, 8), (1, 0, 8), (2, 0, 4), (2, 4, 4))[i])) for side in range(2) for i, ref in enumerate(refs[side * 5 : side * 5 + 5])]
    me = ((lax.axis_index("z") * 4) + lax.axis_index("x")) * 2 + lax.axis_index("core")
    core = lax.axis_index("core")

    at = 0
    for ref, _, _, _, size in blocks:
        for z in range(size):
            for kind, table in enumerate((plain.at[0], plain.at[1], wanted)):
                rows = ref[z, T_AT + kind * LIST_ROWS : T_AT + (kind + 1) * LIST_ROWS, :]
                table[at : at + LIST_ROWS, :] = rows
            at += LIST_ROWS
    for kind in range(2):
        names[:, kind * TB : (kind + 1) * TB] = plain[kind].astype(jnp.bfloat16)

    upto = lax.broadcasted_iota(jnp.int32, (TB, TB), 0) <= lax.broadcasted_iota(jnp.int32, (TB, TB), 1)
    upto = upto.astype(jnp.bfloat16)
    ones = jnp.ones((8, TB), jnp.bfloat16)

    def pick(base):
        hits = []
        for t in range(TILES):
            hit = wanted[...] == (me * TILES + t).astype(jnp.float32)
            hits.append(hit.astype(jnp.float32).astype(jnp.bfloat16))
        totals = [dot(ones, hit, NT) for hit in hits]
        for t in range(TILES):
            place = dot(hits[t], upto)
            names[:, (2 + t) * TB : (3 + t) * TB] = place.astype(jnp.bfloat16) * hits[t]
        lowers, uppers, sums = [], [], []
        for t in range(TILES):
            carry = jnp.zeros((8, 1), jnp.float32)
            upper = []
            for i in range(0, LISTS, TB):
                piece = totals[t][:, i : i + TB].astype(jnp.bfloat16)
                within = dot(piece, upto[: piece.shape[1], : piece.shape[1]])
                upper.append(within + carry)
                carry = carry + within[:, -1:]
            uppers.append(jnp.concatenate(upper, axis=1))
            lowers.append(uppers[t] - totals[t])
            sums.append(carry)
        rank = (base + lax.broadcasted_iota(jnp.int32, (CHUNK, LISTS), 0)).astype(jnp.float32)
        entry = (base + lax.broadcasted_iota(jnp.int32, (8, CHUNK), 1)).astype(jnp.float32)
        rows = [(lowers[t][0:1] <= rank) & (rank < uppers[t][0:1]) for t in range(TILES)]
        before = [jnp.sum(jnp.where(rows[t], lowers[t][0:1], 0.0), axis=1, keepdims=True) for t in range(TILES)]
        rows = [row.astype(jnp.float32).astype(jnp.bfloat16) for row in rows]
        found = [dot(rows[t], names[:, 0 : 2 * TB]) for t in range(TILES)]
        places = [dot(rows[t], names[:, (2 + t) * TB : (3 + t) * TB]) for t in range(TILES)]
        for t in range(TILES):
            chosen = places[t] == rank[:, 0:1] + 1.0 - before[t]
            left = dot(ones, jnp.where(chosen, found[t][:, 0:TB], 0.0).astype(jnp.bfloat16), NT)
            right = dot(ones, jnp.where(chosen, found[t][:, TB : 2 * TB], 0.0).astype(jnp.bfloat16), NT)
            code = jnp.where(entry < sums[t], left * 256.0 + right, float(ALL_TILES * 256))
            lists_v[t : t + 1, 0:CHUNK] = code[0:1].astype(jnp.int32)
            lists_v[t : t + 1, CHUNK:] = jnp.full((1, WIDTH - CHUNK), ALL_TILES * 256, jnp.int32)
            lists_v[TILES + t : TILES + t + 1, :] = jnp.broadcast_to(sums[t][0:1], (1, WIDTH)).astype(jnp.int32)

    def spread(index, _):
        for ref, side, step, first, size in blocks:
            if size == 4:
                ref = ref.at[pl.ds(index // 2, 1)]
            else:
                ref = ref.at[pl.ds(index, 1)]
            z = index // 2 + first if size == 4 else index
            c = core if side == 0 else 1 - core
            owner = (z * 4 + (my_x + step) % 4) * 2 + c
            to = pl.ds(pl.multiple_of(owner * TILES * KS, TILES * KS), TILES * KS)
            for at, store in ((A_AT, sa), (B_AT, sb)):
                value = ref[0, at : at + TILES * KS, :]
                high = value.astype(jnp.bfloat16)
                store[to, 0:TB] = high
                store[to, TB : 2 * TB] = (value - high.astype(jnp.float32)).astype(jnp.bfloat16)
        return 0

    def one_round(state):
        turn, _ = state
        base = turn * CHUNK
        pick(base)
        copy = pltpu.make_async_copy(lists_v, lists_s, sem)
        copy.start()

        @pl.when(turn == 0)
        def _():
            lax.fori_loop(0, 8, spread, 0)
            sa[ALL_TILES * KS :, :] = jnp.zeros((KS, 2 * TB), jnp.bfloat16)
            acc[...] = jnp.zeros_like(acc)

        copy.wait()
        most, starts = jnp.int32(0), [jnp.int32(0)]
        for t in range(TILES):
            total = lists_s[TILES + t, 0]
            most = jnp.maximum(most, total)
            starts.append(starts[t] + (jnp.clip(total - base, 0, CHUNK) + SUB - 1) // SUB)

        def block(index, _):
            targets, sums = [], []
            for u in range(WAYS):
                at = index * WAYS + u
                t = (at >= starts[1]).astype(jnp.int32) + (at >= starts[2]).astype(jnp.int32) + (at >= starts[3]).astype(jnp.int32)
                first = jnp.where(t == 0, 0, jnp.where(t == 1, starts[1], jnp.where(t == 2, starts[2], starts[3])))
                first = (at - first) * SUB
                targets.append(t)
                lefts, rights = [], []
                for i in range(SUB):
                    code = lists_s[t, first + i]
                    a = pl.multiple_of((code >> 8) * KS, KS)
                    b = pl.multiple_of((code & 255) * KS, KS)
                    lefts.append(sa[pl.ds(a, KS), :])
                    rights.append(sb[pl.ds(b, KS), :])
                sums.append(dot(jnp.concatenate(lefts, axis=0), jnp.concatenate(rights, axis=0), TN))
            for u in range(WAYS):
                acc[targets[u]] += sums[u]
            return 0

        lax.fori_loop(0, (starts[TILES] + WAYS - 1) // WAYS, block, 0)
        return turn + 1, (most + CHUNK - 1) // CHUNK

    lax.while_loop(lambda s: s[0] < s[1], one_round, (jnp.int32(0), jnp.int32(1)))
    for t in range(TILES):
        total = (acc[t, 0:TB, 0:TB] + acc[t, 0:TB, TB:]) + (acc[t, TB:, 0:TB] + acc[t, TB:, TB:])
        for m in range(MEMBERS):
            out_ref[m, t] = total[m * KS : (m + 1) * KS, :]


VMEM = pl.BlockSpec(memory_space=pltpu.VMEM)
SMEM = pl.BlockSpec(memory_space=pltpu.SMEM)
PARAMS = pltpu.CompilerParams(vmem_limit_bytes=48 * 1024 * 1024)


def shift(block, by):
    return lax.ppermute(block, "x", [(i, (i + by) % 4) for i in range(4)])


def swap(block, axis):
    return lax.all_to_all(block, axis, split_axis=0, concat_axis=0, tiled=True)


def local(amplitudes, integrals, residual_in, task_lists, task_counts, amp_wanted, int_wanted, res_targets):
    f32 = jnp.float32
    lists = pl.pallas_call(
        task_kernel,
        out_shape=pltpu.VMEM((MEMBERS, 3, TB), f32),
        in_specs=[VMEM, SMEM, VMEM, VMEM, VMEM],
        out_specs=VMEM,
    )(task_lists.transpose(0, 3, 1, 2), task_counts, amp_wanted, int_wanted, res_targets)
    lists = swap(lists, "grp")
    tiles = pl.pallas_call(
        turn_kernel,
        out_shape=pltpu.VMEM((T_AT, TB), f32),
        in_specs=[VMEM] * 2,
        out_specs=VMEM,
        scratch_shapes=[pltpu.VMEM((TILES, TB, TB), f32)],
    )(amplitudes, integrals)
    payload = pl.pallas_call(
        payload_kernel,
        out_shape=pltpu.VMEM((8, ROWS, TB), f32),
        in_specs=[SMEM, VMEM, VMEM],
        out_specs=VMEM,
        scratch_shapes=[pltpu.VMEM((MEMBERS, 3, TB), f32)],
    )(task_counts, pltpu.with_memory_space_constraint(tiles, pltpu.VMEM), pltpu.with_memory_space_constraint(lists, pltpu.VMEM))
    here = swap(payload, "z")
    left, right = shift(here, 1), shift(here, -1)
    near = [here, left, right, shift(left[:4], 1), shift(right[4:], -1)]
    far = [lax.ppermute(block, "core", [(0, 1), (1, 0)]) for block in near]
    bf16 = jnp.bfloat16
    partial = pl.pallas_call(
        ladder_kernel,
        out_shape=pltpu.VMEM((MEMBERS, TILES, KS, TB), f32),
        in_specs=[VMEM] * 10,
        out_specs=VMEM,
        scratch_shapes=[
            pltpu.VMEM(((ALL_TILES + 1) * KS, 2 * TB), bf16),
            pltpu.VMEM((ALL_TILES * KS, 2 * TB), bf16),
            pltpu.VMEM((TILES, 2 * TB, 2 * TB), f32),
            pltpu.VMEM((LISTS, TB), f32),
            pltpu.VMEM((2, LISTS, TB), f32),
            pltpu.VMEM((LISTS, (2 + TILES) * TB), bf16),
            pltpu.VMEM((2 * TILES, WIDTH), jnp.int32),
            pltpu.SMEM((2 * TILES, WIDTH), jnp.int32),
            pltpu.SemaphoreType.DMA,
        ],
        compiler_params=PARAMS,
    )(*near, *far)
    member = lax.axis_index("grp")
    rows = lax.dynamic_slice_in_dim(residual_in, member * KS, KS, 1)
    rows = rows + jnp.sum(swap(partial, "grp"), axis=0)
    whole = swap(jnp.broadcast_to(rows[None], (MEMBERS, TILES, KS, TB)), "grp")
    return whole.transpose(1, 0, 2, 3).reshape(TILES, TB, TB)


def solution(mesh):
    fine = Mesh(mesh.devices.reshape(8, 4, 2, MEMBERS), ("z", "x", "core", "grp"))
    wide = ("z", "x", "core")
    placed = (
        P(wide, None, None),
        P(wide, None, None),
        P(wide, None, None),
        P(wide, "grp", None, None),
        P(wide, None),
        P(wide, None),
        P(wide, None),
        P(wide, None),
    )
    return jax.shard_map(local, mesh=fine, in_specs=placed, out_specs=P(wide, None, None), check_vma=False)
```

```python
import jax
import jax.numpy as jnp
from jax import lax
from jax.experimental import pallas as pl
from jax.experimental.pallas import tpu as pltpu
from jax.sharding import Mesh, PartitionSpec as P

TB = 128
TILES = 4
OWNERS = 64
MEMBERS = 8
KS = TB // MEMBERS
ALL_TILES = OWNERS * TILES
ROWS = 2 * TILES * KS + 16
LIST_ROWS = 5
A_AT, B_AT, T_AT = 0, TILES * KS, 2 * TILES * KS
LISTS = OWNERS * LIST_ROWS
CHUNK = 288
SUB = 32
WAYS = 3
WIDTH = CHUNK + 96

NT = (((1,), (1,)), ((), ()))
TN = (((0,), (0,)), ((), ()))


def dot(a, b, dims=(((1,), (0,)), ((), ()))):
    return lax.dot_general(a, b, dims, preferred_element_type=jnp.float32)


def task_kernel(tasks_ref, counts_ref, amp_ref, int_ref, res_ref, out_ref):
    live = counts_ref[0, lax.axis_index("grp")]
    owner = lax.broadcasted_iota(jnp.int32, (OWNERS, TB), 0)
    slot = lax.broadcasted_iota(jnp.int32, (OWNERS, TB), 1)
    number = lax.broadcasted_iota(jnp.int32, (8, OWNERS), 1) * TILES
    for kind, table in enumerate((amp_ref, int_ref, res_ref)):
        hit = tasks_ref[0, kind] == owner
        if kind == 2:
            hit = hit & (slot < live)
        names = number + table[0:1, :] + (1 if kind == 2 else 0)
        row = dot(names.astype(jnp.bfloat16), hit.astype(jnp.bfloat16))[0:1]
        row = row - 1.0 if kind == 2 else row
        for m in range(MEMBERS):
            out_ref[m, kind : kind + 1, :] = row


def turn_kernel(amp_ref, int_ref, out_ref, turned):
    first = pl.multiple_of(lax.axis_index("grp") * KS, KS)
    for at, tiles in ((A_AT, amp_ref), (B_AT, int_ref)):
        for t in range(TILES):
            turned[t] = tiles[t].T
        for t in range(TILES):
            out_ref[at + t * KS : at + (t + 1) * KS, :] = turned[t, pl.ds(first, KS), :]


def payload_kernel(counts_ref, tiles_ref, lists_ref, out_ref, joined):
    joined[...] = jnp.full_like(joined, -1.0)
    lane = lax.broadcasted_iota(jnp.int32, (3, TB), 1)
    at = jnp.int32(0)
    for m in range(MEMBERS):
        row, by = at // TB, at % TB
        turned = pltpu.roll(lists_ref[m], by, 1)
        joined[row] = jnp.where(lane >= by, turned, joined[row])
        joined[row + 1] = jnp.where(lane < by, turned, joined[row + 1])
        at = at + counts_ref[0, m]
    rows = [joined[i, kind : kind + 1, :] for kind in range(3) for i in range(LIST_ROWS)]
    rows = jnp.concatenate(rows + [jnp.zeros((1, TB), jnp.float32)], axis=0)
    for z in range(8):
        out_ref[z, 0:T_AT, :] = tiles_ref[...]
        out_ref[z, T_AT:ROWS, :] = rows


def ladder_kernel(*refs):
    blocks, (out_ref, sa, sb, acc, wanted, plain, names, lists_v, lists_s, sem) = refs[:8], refs[8:]
    me = ((lax.axis_index("z") * 4) + lax.axis_index("x")) * 2 + lax.axis_index("core")
    core = lax.axis_index("core")
    my_x = lax.axis_index("x")

    at = 0
    for ref in blocks:
        for z in range(8):
            for kind, table in enumerate((plain.at[0], plain.at[1], wanted)):
                rows = ref[z, T_AT + kind * LIST_ROWS : T_AT + (kind + 1) * LIST_ROWS, :]
                table[at : at + LIST_ROWS, :] = rows
            at += LIST_ROWS
    for kind in range(2):
        names[:, kind * TB : (kind + 1) * TB] = plain[kind].astype(jnp.bfloat16)

    upto = lax.broadcasted_iota(jnp.int32, (TB, TB), 0) <= lax.broadcasted_iota(jnp.int32, (TB, TB), 1)
    upto = upto.astype(jnp.bfloat16)
    ones = jnp.ones((8, TB), jnp.bfloat16)

    def pick(base):
        hits = []
        for t in range(TILES):
            hit = wanted[...] == (me * TILES + t).astype(jnp.float32)
            hits.append(hit.astype(jnp.float32).astype(jnp.bfloat16))
        totals = [dot(ones, hit, NT) for hit in hits]
        for t in range(TILES):
            place = dot(hits[t], upto)
            names[:, (2 + t) * TB : (3 + t) * TB] = place.astype(jnp.bfloat16) * hits[t]
        lowers, uppers, sums = [], [], []
        for t in range(TILES):
            carry = jnp.zeros((8, 1), jnp.float32)
            upper = []
            for i in range(0, LISTS, TB):
                piece = totals[t][:, i : i + TB].astype(jnp.bfloat16)
                within = dot(piece, upto[: piece.shape[1], : piece.shape[1]])
                upper.append(within + carry)
                carry = carry + within[:, -1:]
            uppers.append(jnp.concatenate(upper, axis=1))
            lowers.append(uppers[t] - totals[t])
            sums.append(carry)
        rank = (base + lax.broadcasted_iota(jnp.int32, (CHUNK, LISTS), 0)).astype(jnp.float32)
        entry = (base + lax.broadcasted_iota(jnp.int32, (8, CHUNK), 1)).astype(jnp.float32)
        rows = [(lowers[t][0:1] <= rank) & (rank < uppers[t][0:1]) for t in range(TILES)]
        before = [jnp.sum(jnp.where(rows[t], lowers[t][0:1], 0.0), axis=1, keepdims=True) for t in range(TILES)]
        rows = [row.astype(jnp.float32).astype(jnp.bfloat16) for row in rows]
        found = [dot(rows[t], names[:, 0 : 2 * TB]) for t in range(TILES)]
        places = [dot(rows[t], names[:, (2 + t) * TB : (3 + t) * TB]) for t in range(TILES)]
        for t in range(TILES):
            chosen = places[t] == rank[:, 0:1] + 1.0 - before[t]
            left = dot(ones, jnp.where(chosen, found[t][:, 0:TB], 0.0).astype(jnp.bfloat16), NT)
            right = dot(ones, jnp.where(chosen, found[t][:, TB : 2 * TB], 0.0).astype(jnp.bfloat16), NT)
            code = jnp.where(entry < sums[t], left * 256.0 + right, float(ALL_TILES * 256))
            lists_v[t : t + 1, 0:CHUNK] = code[0:1].astype(jnp.int32)
            lists_v[t : t + 1, CHUNK:] = jnp.full((1, WIDTH - CHUNK), ALL_TILES * 256, jnp.int32)
            lists_v[TILES + t : TILES + t + 1, :] = jnp.broadcast_to(sums[t][0:1], (1, WIDTH)).astype(jnp.int32)

    def spread(z):
        for i, ref in enumerate(blocks):
            c = core if i < 4 else 1 - core
            owner = (z * 4 + (my_x + (0, 3, 1, 2)[i % 4]) % 4) * 2 + c
            to = pl.ds(pl.multiple_of(owner * TILES * KS, TILES * KS), TILES * KS)
            for at, store in ((A_AT, sa), (B_AT, sb)):
                value = ref[z, at : at + TILES * KS, :]
                if store is sa:
                    store[to, :] = value
                    continue
                high = value.astype(jnp.bfloat16)
                store[to, 0:TB] = high
                store[to, TB : 2 * TB] = (value - high.astype(jnp.float32)).astype(jnp.bfloat16)

    def one_round(state):
        turn, _ = state
        base = turn * CHUNK
        pick(base)
        copy = pltpu.make_async_copy(lists_v, lists_s, sem)
        copy.start()

        @pl.when(turn == 0)
        def _():
            for z in range(8):
                spread(z)
            sa[ALL_TILES * KS :, :] = jnp.zeros((KS, TB), jnp.float32)
            acc[...] = jnp.zeros_like(acc)

        copy.wait()
        most, starts = jnp.int32(0), [jnp.int32(0)]
        for t in range(TILES):
            total = lists_s[TILES + t, 0]
            most = jnp.maximum(most, total)
            starts.append(starts[t] + (jnp.clip(total - base, 0, CHUNK) + SUB - 1) // SUB)

        def block(index, _):
            targets, sums = [], []
            for u in range(WAYS):
                at = index * WAYS + u
                t = (at >= starts[1]).astype(jnp.int32) + (at >= starts[2]).astype(jnp.int32) + (at >= starts[3]).astype(jnp.int32)
                first = jnp.where(t == 0, 0, jnp.where(t == 1, starts[1], jnp.where(t == 2, starts[2], starts[3])))
                first = (at - first) * SUB
                targets.append(t)
                lefts, rights = [], []
                for i in range(SUB):
                    code = lists_s[t, first + i]
                    a = pl.multiple_of((code >> 8) * KS, KS)
                    b = pl.multiple_of((code & 255) * KS, KS)
                    lefts.append(sa[pl.ds(a, KS), :])
                    rights.append(sb[pl.ds(b, KS), :])
                turned = jnp.concatenate(lefts, axis=0).T
                high = turned.astype(jnp.bfloat16)
                turned = jnp.concatenate([high, (turned - high.astype(jnp.float32)).astype(jnp.bfloat16)], axis=0)
                sums.append(dot(turned, jnp.concatenate(rights, axis=0)))
            for u in range(WAYS):
                acc[targets[u]] += sums[u]
            return 0

        lax.fori_loop(0, (starts[TILES] + WAYS - 1) // WAYS, block, 0)
        return turn + 1, (most + CHUNK - 1) // CHUNK

    lax.while_loop(lambda s: s[0] < s[1], one_round, (jnp.int32(0), jnp.int32(1)))
    for t in range(TILES):
        total = (acc[t, 0:TB, 0:TB] + acc[t, 0:TB, TB:]) + (acc[t, TB:, 0:TB] + acc[t, TB:, TB:])
        for half in range(2):
            out_ref[2 * t + half] = total[half * TB // 2 : (half + 1) * TB // 2, :]


VMEM = pl.BlockSpec(memory_space=pltpu.VMEM)
SMEM = pl.BlockSpec(memory_space=pltpu.SMEM)
PARAMS = pltpu.CompilerParams(vmem_limit_bytes=48 * 1024 * 1024)


def shift(block, by):
    return lax.ppermute(block, "x", [(i, (i + by) % 4) for i in range(4)])


def across(block):
    return lax.ppermute(block, "core", [(0, 1), (1, 0)])


def swap(block, axis):
    return lax.all_to_all(block, axis, split_axis=0, concat_axis=0, tiled=True)


def local(amplitudes, integrals, residual_in, task_lists, task_counts, amp_wanted, int_wanted, res_targets):
    f32 = jnp.float32
    lists = pl.pallas_call(
        task_kernel,
        out_shape=pltpu.VMEM((MEMBERS, 3, TB), f32),
        in_specs=[VMEM, SMEM, VMEM, VMEM, VMEM],
        out_specs=VMEM,
    )(task_lists.transpose(0, 3, 1, 2), task_counts, amp_wanted, int_wanted, res_targets)
    lists = swap(lists, "grp")
    tiles = pl.pallas_call(
        turn_kernel,
        out_shape=pltpu.VMEM((T_AT, TB), f32),
        in_specs=[VMEM] * 2,
        out_specs=VMEM,
        scratch_shapes=[pltpu.VMEM((TILES, TB, TB), f32)],
    )(amplitudes, integrals)
    payload = pl.pallas_call(
        payload_kernel,
        out_shape=pltpu.VMEM((8, ROWS, TB), f32),
        in_specs=[SMEM, VMEM, VMEM],
        out_specs=VMEM,
        scratch_shapes=[pltpu.VMEM((MEMBERS, 3, TB), f32)],
    )(task_counts, pltpu.with_memory_space_constraint(tiles, pltpu.VMEM), pltpu.with_memory_space_constraint(lists, pltpu.VMEM))
    here = swap(payload, "z")
    left, right, here_far = shift(here, 1), shift(here, -1), across(here)
    ahead, behind, here_far = lax.optimization_barrier((shift(left[:4], 1), shift(right[4:], -1), here_far))
    opposite = jnp.concatenate([ahead, behind])
    near = [here, left, right, opposite]
    far = [here_far, across(left), across(right), across(opposite)]
    bf16 = jnp.bfloat16
    partial = pl.pallas_call(
        ladder_kernel,
        out_shape=pltpu.VMEM((MEMBERS, TB // 2, TB), f32),
        in_specs=[VMEM] * 8,
        out_specs=VMEM,
        scratch_shapes=[
            pltpu.VMEM(((ALL_TILES + 1) * KS, TB), f32),
            pltpu.VMEM((ALL_TILES * KS, 2 * TB), bf16),
            pltpu.VMEM((TILES, 2 * TB, 2 * TB), f32),
            pltpu.VMEM((LISTS, TB), f32),
            pltpu.VMEM((2, LISTS, TB), f32),
            pltpu.VMEM((LISTS, (2 + TILES) * TB), bf16),
            pltpu.VMEM((2 * TILES, WIDTH), jnp.int32),
            pltpu.SMEM((2 * TILES, WIDTH), jnp.int32),
            pltpu.SemaphoreType.DMA,
        ],
        compiler_params=PARAMS,
    )(*near, *far)
    halves = residual_in.reshape(MEMBERS, TB // 2, TB)
    half = lax.dynamic_index_in_dim(halves, lax.axis_index("grp"), 0, keepdims=False)
    half = half + jnp.sum(swap(partial, "grp"), axis=0)
    whole = swap(jnp.broadcast_to(half[None], halves.shape), "grp")
    return whole.reshape(TILES, TB, TB)


def solution(mesh):
    fine = Mesh(mesh.devices.reshape(8, 4, 2, MEMBERS), ("z", "x", "core", "grp"))
    wide = ("z", "x", "core")
    placed = (
        P(wide, None, None),
        P(wide, None, None),
        P(wide, None, None),
        P(wide, "grp", None, None),
        P(wide, None),
        P(wide, None),
        P(wide, None),
        P(wide, None),
    )
    return jax.shard_map(local, mesh=fine, in_specs=placed, out_specs=P(wide, None, None), check_vma=False)
```

```python
import jax
import jax.numpy as jnp
from jax import lax
from jax.experimental import pallas as pl
from jax.experimental.pallas import tpu as pltpu
from jax.sharding import Mesh, PartitionSpec as P

TB = 128
TILES = 4
OWNERS = 64
MEMBERS = 8
KS = TB // MEMBERS
ALL_TILES = OWNERS * TILES
ROWS = 2 * TILES * KS + 16
LIST_ROWS = 5
A_AT, B_AT, T_AT = 0, TILES * KS, 2 * TILES * KS
LISTS = OWNERS * LIST_ROWS
CHUNK = 288
SUB = 32
WAYS = 3
WIDTH = CHUNK + 96

NT = (((1,), (1,)), ((), ()))
TN = (((0,), (0,)), ((), ()))


def dot(a, b, dims=(((1,), (0,)), ((), ()))):
    return lax.dot_general(a, b, dims, preferred_element_type=jnp.float32)


def task_kernel(tasks_ref, counts_ref, amp_ref, int_ref, res_ref, out_ref):
    live = counts_ref[0, lax.axis_index("grp")]
    owner = lax.broadcasted_iota(jnp.int32, (OWNERS, TB), 0)
    slot = lax.broadcasted_iota(jnp.int32, (OWNERS, TB), 1)
    number = lax.broadcasted_iota(jnp.int32, (8, OWNERS), 1) * TILES
    for kind, table in enumerate((amp_ref, int_ref, res_ref)):
        hit = tasks_ref[0, kind] == owner
        if kind == 2:
            hit = hit & (slot < live)
        names = number + table[0:1, :] + (1 if kind == 2 else 0)
        row = dot(names.astype(jnp.bfloat16), hit.astype(jnp.bfloat16))[0:1]
        row = row - 1.0 if kind == 2 else row
        for m in range(MEMBERS):
            out_ref[m, kind : kind + 1, :] = row


def turn_kernel(amp_ref, int_ref, out_ref, turned):
    first = pl.multiple_of(lax.axis_index("grp") * KS, KS)
    for at, tiles in ((A_AT, amp_ref), (B_AT, int_ref)):
        for t in range(TILES):
            turned[t] = tiles[t].T
        for t in range(TILES):
            out_ref[at + t * KS : at + (t + 1) * KS, :] = turned[t, pl.ds(first, KS), :]


def payload_kernel(counts_ref, tiles_ref, lists_ref, out_ref, joined):
    joined[...] = jnp.full_like(joined, -1.0)
    lane = lax.broadcasted_iota(jnp.int32, (3, TB), 1)
    at = jnp.int32(0)
    for m in range(MEMBERS):
        row, by = at // TB, at % TB
        turned = pltpu.roll(lists_ref[m], by, 1)
        joined[row] = jnp.where(lane >= by, turned, joined[row])
        joined[row + 1] = jnp.where(lane < by, turned, joined[row + 1])
        at = at + counts_ref[0, m]
    rows = [joined[i, kind : kind + 1, :] for kind in range(3) for i in range(LIST_ROWS)]
    rows = jnp.concatenate(rows + [jnp.zeros((1, TB), jnp.float32)], axis=0)
    for z in range(8):
        out_ref[z, 0:T_AT, :] = tiles_ref[...]
        out_ref[z, T_AT:ROWS, :] = rows


def ladder_kernel(*refs):
    parts, (out_ref, sa, sb, acc, wanted, plain, names, lists_v, lists_s, sem) = refs[:10], refs[10:]
    blocks = [[[ref.at[z] for z in range(8)] for ref in parts[i : i + 3]] + [[parts[i + 3 + z // 4].at[z % 4] for z in range(8)]] for i in (0, 5)]
    blocks = blocks[0] + blocks[1]
    me = ((lax.axis_index("z") * 4) + lax.axis_index("x")) * 2 + lax.axis_index("core")
    core = lax.axis_index("core")
    my_x = lax.axis_index("x")

    at = 0
    for ref in blocks:
        for z in range(8):
            for kind, table in enumerate((plain.at[0], plain.at[1], wanted)):
                rows = ref[z][T_AT + kind * LIST_ROWS : T_AT + (kind + 1) * LIST_ROWS, :]
                table[at : at + LIST_ROWS, :] = rows
            at += LIST_ROWS
    for kind in range(2):
        names[:, kind * TB : (kind + 1) * TB] = plain[kind].astype(jnp.bfloat16)

    upto = lax.broadcasted_iota(jnp.int32, (TB, TB), 0) <= lax.broadcasted_iota(jnp.int32, (TB, TB), 1)
    upto = upto.astype(jnp.bfloat16)
    ones = jnp.ones((8, TB), jnp.bfloat16)

    def pick(base):
        hits = []
        for t in range(TILES):
            hit = wanted[...] == (me * TILES + t).astype(jnp.float32)
            hits.append(hit.astype(jnp.float32).astype(jnp.bfloat16))
        totals = [dot(ones, hit, NT) for hit in hits]
        for t in range(TILES):
            place = dot(hits[t], upto)
            names[:, (2 + t) * TB : (3 + t) * TB] = place.astype(jnp.bfloat16) * hits[t]
        lowers, uppers, sums = [], [], []
        for t in range(TILES):
            carry = jnp.zeros((8, 1), jnp.float32)
            upper = []
            for i in range(0, LISTS, TB):
                piece = totals[t][:, i : i + TB].astype(jnp.bfloat16)
                within = dot(piece, upto[: piece.shape[1], : piece.shape[1]])
                upper.append(within + carry)
                carry = carry + within[:, -1:]
            uppers.append(jnp.concatenate(upper, axis=1))
            lowers.append(uppers[t] - totals[t])
            sums.append(carry)
        rank = (base + lax.broadcasted_iota(jnp.int32, (CHUNK, LISTS), 0)).astype(jnp.float32)
        entry = (base + lax.broadcasted_iota(jnp.int32, (8, CHUNK), 1)).astype(jnp.float32)
        rows = [(lowers[t][0:1] <= rank) & (rank < uppers[t][0:1]) for t in range(TILES)]
        before = [jnp.sum(jnp.where(rows[t], lowers[t][0:1], 0.0), axis=1, keepdims=True) for t in range(TILES)]
        rows = [row.astype(jnp.float32).astype(jnp.bfloat16) for row in rows]
        found = [dot(rows[t], names[:, 0 : 2 * TB]) for t in range(TILES)]
        places = [dot(rows[t], names[:, (2 + t) * TB : (3 + t) * TB]) for t in range(TILES)]
        for t in range(TILES):
            chosen = places[t] == rank[:, 0:1] + 1.0 - before[t]
            left = dot(ones, jnp.where(chosen, found[t][:, 0:TB], 0.0).astype(jnp.bfloat16), NT)
            right = dot(ones, jnp.where(chosen, found[t][:, TB : 2 * TB], 0.0).astype(jnp.bfloat16), NT)
            code = jnp.where(entry < sums[t], left * 256.0 + right, float(ALL_TILES * 256))
            lists_v[t : t + 1, 0:CHUNK] = code[0:1].astype(jnp.int32)
            lists_v[t : t + 1, CHUNK:] = jnp.full((1, WIDTH - CHUNK), ALL_TILES * 256, jnp.int32)
            lists_v[TILES + t : TILES + t + 1, :] = jnp.broadcast_to(sums[t][0:1], (1, WIDTH)).astype(jnp.int32)

    def spread(z):
        for i, ref in enumerate(blocks):
            c = core if i < 4 else 1 - core
            owner = (z * 4 + (my_x + (0, 3, 1, 2)[i % 4]) % 4) * 2 + c
            to = pl.ds(pl.multiple_of(owner * TILES * KS, TILES * KS), TILES * KS)
            for at, store in ((A_AT, sa), (B_AT, sb)):
                value = ref[z][at : at + TILES * KS, :]
                if store is sa:
                    store[to, :] = value
                    continue
                high = value.astype(jnp.bfloat16)
                store[to, 0:TB] = high
                store[to, TB : 2 * TB] = (value - high.astype(jnp.float32)).astype(jnp.bfloat16)

    def one_round(state):
        turn, _ = state
        base = turn * CHUNK
        pick(base)
        copy = pltpu.make_async_copy(lists_v, lists_s, sem)
        copy.start()

        @pl.when(turn == 0)
        def _():
            for z in range(8):
                spread(z)
            sa[ALL_TILES * KS :, :] = jnp.zeros((KS, TB), jnp.float32)
            acc[...] = jnp.zeros_like(acc)

        copy.wait()
        most, starts = jnp.int32(0), [jnp.int32(0)]
        for t in range(TILES):
            total = lists_s[TILES + t, 0]
            most = jnp.maximum(most, total)
            starts.append(starts[t] + (jnp.clip(total - base, 0, CHUNK) + SUB - 1) // SUB)

        def block(index, _):
            targets, sums = [], []
            for u in range(WAYS):
                at = index * WAYS + u
                t = (at >= starts[1]).astype(jnp.int32) + (at >= starts[2]).astype(jnp.int32) + (at >= starts[3]).astype(jnp.int32)
                first = jnp.where(t == 0, 0, jnp.where(t == 1, starts[1], jnp.where(t == 2, starts[2], starts[3])))
                first = (at - first) * SUB
                targets.append(t)
                lefts, rights = [], []
                for i in range(SUB):
                    code = lists_s[t, first + i]
                    a = pl.multiple_of((code >> 8) * KS, KS)
                    b = pl.multiple_of((code & 255) * KS, KS)
                    lefts.append(sa[pl.ds(a, KS), :])
                    rights.append(sb[pl.ds(b, KS), :])
                turned = jnp.concatenate(lefts, axis=0).T
                high = turned.astype(jnp.bfloat16)
                turned = jnp.concatenate([high, (turned - high.astype(jnp.float32)).astype(jnp.bfloat16)], axis=0)
                sums.append(dot(turned, jnp.concatenate(rights, axis=0)))
            for u in range(WAYS):
                acc[targets[u]] += sums[u]
            return 0

        lax.fori_loop(0, (starts[TILES] + WAYS - 1) // WAYS, block, 0)
        return turn + 1, (most + CHUNK - 1) // CHUNK

    lax.while_loop(lambda s: s[0] < s[1], one_round, (jnp.int32(0), jnp.int32(1)))
    for t in range(TILES):
        total = (acc[t, 0:TB, 0:TB] + acc[t, 0:TB, TB:]) + (acc[t, TB:, 0:TB] + acc[t, TB:, TB:])
        for half in range(2):
            out_ref[2 * t + half] = total[half * TB // 2 : (half + 1) * TB // 2, :]


VMEM = pl.BlockSpec(memory_space=pltpu.VMEM)
SMEM = pl.BlockSpec(memory_space=pltpu.SMEM)
PARAMS = pltpu.CompilerParams(vmem_limit_bytes=48 * 1024 * 1024)


def shift(block, by):
    return lax.ppermute(block, "x", [(i, (i + by) % 4) for i in range(4)])


def across(block):
    return lax.ppermute(block, "core", [(0, 1), (1, 0)])


def swap(block, axis):
    return lax.all_to_all(block, axis, split_axis=0, concat_axis=0, tiled=True)


def local(amplitudes, integrals, residual_in, task_lists, task_counts, amp_wanted, int_wanted, res_targets):
    f32 = jnp.float32
    lists = pl.pallas_call(
        task_kernel,
        out_shape=pltpu.VMEM((MEMBERS, 3, TB), f32),
        in_specs=[VMEM, SMEM, VMEM, VMEM, VMEM],
        out_specs=VMEM,
    )(task_lists.transpose(0, 3, 1, 2), task_counts, amp_wanted, int_wanted, res_targets)
    lists = swap(lists, "grp")
    tiles = pl.pallas_call(
        turn_kernel,
        out_shape=pltpu.VMEM((T_AT, TB), f32),
        in_specs=[VMEM] * 2,
        out_specs=VMEM,
        scratch_shapes=[pltpu.VMEM((TILES, TB, TB), f32)],
    )(amplitudes, integrals)
    payload = pl.pallas_call(
        payload_kernel,
        out_shape=pltpu.VMEM((8, ROWS, TB), f32),
        in_specs=[SMEM, VMEM, VMEM],
        out_specs=VMEM,
        scratch_shapes=[pltpu.VMEM((MEMBERS, 3, TB), f32)],
    )(task_counts, pltpu.with_memory_space_constraint(tiles, pltpu.VMEM), pltpu.with_memory_space_constraint(lists, pltpu.VMEM))
    here = swap(payload, "z")
    left, right = shift(here, 1), shift(here, -1)
    near = [here, left, right, shift(left[:4], 1), shift(right[4:], -1)]
    far = [across(block) for block in near]
    bf16 = jnp.bfloat16
    partial = pl.pallas_call(
        ladder_kernel,
        out_shape=pltpu.VMEM((MEMBERS, TB // 2, TB), f32),
        in_specs=[VMEM] * 10,
        out_specs=VMEM,
        scratch_shapes=[
            pltpu.VMEM(((ALL_TILES + 1) * KS, TB), f32),
            pltpu.VMEM((ALL_TILES * KS, 2 * TB), bf16),
            pltpu.VMEM((TILES, 2 * TB, 2 * TB), f32),
            pltpu.VMEM((LISTS, TB), f32),
            pltpu.VMEM((2, LISTS, TB), f32),
            pltpu.VMEM((LISTS, (2 + TILES) * TB), bf16),
            pltpu.VMEM((2 * TILES, WIDTH), jnp.int32),
            pltpu.SMEM((2 * TILES, WIDTH), jnp.int32),
            pltpu.SemaphoreType.DMA,
        ],
        compiler_params=PARAMS,
    )(*near, *far)
    halves = residual_in.reshape(MEMBERS, TB // 2, TB)
    half = lax.dynamic_index_in_dim(halves, lax.axis_index("grp"), 0, keepdims=False)
    half = half + jnp.sum(swap(partial, "grp"), axis=0)
    whole = swap(jnp.broadcast_to(half[None], halves.shape), "grp")
    return whole.reshape(TILES, TB, TB)


def solution(mesh):
    fine = Mesh(mesh.devices.reshape(8, 4, 2, MEMBERS), ("z", "x", "core", "grp"))
    wide = ("z", "x", "core")
    placed = (
        P(wide, None, None),
        P(wide, None, None),
        P(wide, None, None),
        P(wide, "grp", None, None),
        P(wide, None),
        P(wide, None),
        P(wide, None),
        P(wide, None),
    )
    return jax.shard_map(local, mesh=fine, in_specs=placed, out_specs=P(wide, None, None), check_vma=False)
```

```python
import jax
import jax.numpy as jnp
from jax import lax
from jax.experimental import pallas as pl
from jax.experimental.pallas import tpu as pltpu
from jax.sharding import Mesh, PartitionSpec as P

TB = 128
TILES = 4
OWNERS = 64
MEMBERS = 8
KS = TB // MEMBERS
ALL_TILES = OWNERS * TILES
ROWS = 2 * TILES * KS + 16
LIST_ROWS = 5
A_AT, B_AT, T_AT = 0, TILES * KS, 2 * TILES * KS
LISTS = OWNERS * LIST_ROWS
CHUNK = 288
SUB = 32
WAYS = 3
WIDTH = CHUNK + 96

NT = (((1,), (1,)), ((), ()))
TN = (((0,), (0,)), ((), ()))


def dot(a, b, dims=(((1,), (0,)), ((), ()))):
    return lax.dot_general(a, b, dims, preferred_element_type=jnp.float32)


def turn_kernel(amp_ref, int_ref, out_ref, turned):
    first = pl.multiple_of(lax.axis_index("grp") * KS, KS)
    for at, tiles in ((A_AT, amp_ref), (B_AT, int_ref)):
        for t in range(TILES):
            turned[t] = tiles[t].T
        for t in range(TILES):
            out_ref[at + t * KS : at + (t + 1) * KS, :] = turned[t, pl.ds(first, KS), :]


def payload_kernel(counts_ref, tiles_ref, lists_ref, amp_ref, int_ref, res_ref, out_ref, joined):
    owner = lax.broadcasted_iota(jnp.int32, (OWNERS, TB), 0)
    slot = lax.broadcasted_iota(jnp.int32, (OWNERS, TB), 1)
    number = lax.broadcasted_iota(jnp.int32, (8, OWNERS), 1) * TILES

    def named(m):
        rows = []
        for kind, table in enumerate((amp_ref, int_ref, res_ref)):
            hit = lists_ref[m, kind : kind + 1, :] == owner
            if kind == 2:
                hit = hit & (slot < counts_ref[0, m])
            names = number + table[0:1, :] + (1 if kind == 2 else 0)
            row = dot(names.astype(jnp.bfloat16), hit.astype(jnp.bfloat16))[0:1]
            rows.append(row - 1.0 if kind == 2 else row)
        return jnp.concatenate(rows, axis=0)

    lists = [named(m) for m in range(MEMBERS)]
    joined[...] = jnp.full_like(joined, -1.0)
    lane = lax.broadcasted_iota(jnp.int32, (3, TB), 1)
    at = jnp.int32(0)
    for m in range(MEMBERS):
        row, by = at // TB, at % TB
        turned = pltpu.roll(lists[m], by, 1)
        joined[row] = jnp.where(lane >= by, turned, joined[row])
        joined[row + 1] = jnp.where(lane < by, turned, joined[row + 1])
        at = at + counts_ref[0, m]
    rows = [joined[i, kind : kind + 1, :] for kind in range(3) for i in range(LIST_ROWS)]
    rows = jnp.concatenate(rows + [jnp.zeros((1, TB), jnp.float32)], axis=0)
    for z in range(8):
        out_ref[z, 0:T_AT, :] = tiles_ref[...]
        out_ref[z, T_AT:ROWS, :] = rows


def ladder_kernel(*refs):
    blocks, (out_ref, sa, sb, acc, wanted, plain, names, lists_v, lists_s, sem) = refs[:8], refs[8:]
    me = ((lax.axis_index("z") * 4) + lax.axis_index("x")) * 2 + lax.axis_index("core")
    core = lax.axis_index("core")
    my_x = lax.axis_index("x")

    at = 0
    for ref in blocks:
        for z in range(8):
            for kind, table in enumerate((plain.at[0], plain.at[1], wanted)):
                rows = ref[z, T_AT + kind * LIST_ROWS : T_AT + (kind + 1) * LIST_ROWS, :]
                table[at : at + LIST_ROWS, :] = rows
            at += LIST_ROWS
    for kind in range(2):
        names[:, kind * TB : (kind + 1) * TB] = plain[kind].astype(jnp.bfloat16)

    upto = lax.broadcasted_iota(jnp.int32, (TB, TB), 0) <= lax.broadcasted_iota(jnp.int32, (TB, TB), 1)
    upto = upto.astype(jnp.bfloat16)
    ones = jnp.ones((8, TB), jnp.bfloat16)

    def pick(base):
        hits = []
        for t in range(TILES):
            hit = wanted[...] == (me * TILES + t).astype(jnp.float32)
            hits.append(hit.astype(jnp.float32).astype(jnp.bfloat16))
        totals = [dot(ones, hit, NT) for hit in hits]
        for t in range(TILES):
            place = dot(hits[t], upto)
            names[:, (2 + t) * TB : (3 + t) * TB] = place.astype(jnp.bfloat16) * hits[t]
        lowers, uppers, sums = [], [], []
        for t in range(TILES):
            carry = jnp.zeros((8, 1), jnp.float32)
            upper = []
            for i in range(0, LISTS, TB):
                piece = totals[t][:, i : i + TB].astype(jnp.bfloat16)
                within = dot(piece, upto[: piece.shape[1], : piece.shape[1]])
                upper.append(within + carry)
                carry = carry + within[:, -1:]
            uppers.append(jnp.concatenate(upper, axis=1))
            lowers.append(uppers[t] - totals[t])
            sums.append(carry)
        rank = (base + lax.broadcasted_iota(jnp.int32, (CHUNK, LISTS), 0)).astype(jnp.float32)
        entry = (base + lax.broadcasted_iota(jnp.int32, (8, CHUNK), 1)).astype(jnp.float32)
        rows = [(lowers[t][0:1] <= rank) & (rank < uppers[t][0:1]) for t in range(TILES)]
        before = [jnp.sum(jnp.where(rows[t], lowers[t][0:1], 0.0), axis=1, keepdims=True) for t in range(TILES)]
        rows = [row.astype(jnp.float32).astype(jnp.bfloat16) for row in rows]
        found = [dot(rows[t], names[:, 0 : 2 * TB]) for t in range(TILES)]
        places = [dot(rows[t], names[:, (2 + t) * TB : (3 + t) * TB]) for t in range(TILES)]
        for t in range(TILES):
            chosen = places[t] == rank[:, 0:1] + 1.0 - before[t]
            left = dot(ones, jnp.where(chosen, found[t][:, 0:TB], 0.0).astype(jnp.bfloat16), NT)
            right = dot(ones, jnp.where(chosen, found[t][:, TB : 2 * TB], 0.0).astype(jnp.bfloat16), NT)
            code = jnp.where(entry < sums[t], left * 256.0 + right, float(ALL_TILES * 256))
            lists_v[t : t + 1, 0:CHUNK] = code[0:1].astype(jnp.int32)
            lists_v[t : t + 1, CHUNK:] = jnp.full((1, WIDTH - CHUNK), ALL_TILES * 256, jnp.int32)
            lists_v[TILES + t : TILES + t + 1, :] = jnp.broadcast_to(sums[t][0:1], (1, WIDTH)).astype(jnp.int32)

    def spread(z):
        for i, ref in enumerate(blocks):
            c = core if i < 4 else 1 - core
            owner = (z * 4 + (my_x + (0, 3, 1, 2)[i % 4]) % 4) * 2 + c
            to = pl.ds(pl.multiple_of(owner * TILES * KS, TILES * KS), TILES * KS)
            for at, store in ((A_AT, sa), (B_AT, sb)):
                value = ref[z, at : at + TILES * KS, :]
                if store is sa:
                    store[to, :] = value
                    continue
                high = value.astype(jnp.bfloat16)
                store[to, 0:TB] = high
                store[to, TB : 2 * TB] = (value - high.astype(jnp.float32)).astype(jnp.bfloat16)

    def one_round(state):
        turn, _ = state
        base = turn * CHUNK
        pick(base)
        copy = pltpu.make_async_copy(lists_v, lists_s, sem)
        copy.start()

        @pl.when(turn == 0)
        def _():
            for z in range(8):
                spread(z)
            sa[ALL_TILES * KS :, :] = jnp.zeros((KS, TB), jnp.float32)
            acc[...] = jnp.zeros_like(acc)

        copy.wait()
        most, starts = jnp.int32(0), [jnp.int32(0)]
        for t in range(TILES):
            total = lists_s[TILES + t, 0]
            most = jnp.maximum(most, total)
            starts.append(starts[t] + (jnp.clip(total - base, 0, CHUNK) + SUB - 1) // SUB)

        def block(index, _):
            targets, sums = [], []
            for u in range(WAYS):
                at = index * WAYS + u
                t = (at >= starts[1]).astype(jnp.int32) + (at >= starts[2]).astype(jnp.int32) + (at >= starts[3]).astype(jnp.int32)
                first = jnp.where(t == 0, 0, jnp.where(t == 1, starts[1], jnp.where(t == 2, starts[2], starts[3])))
                first = (at - first) * SUB
                targets.append(t)
                lefts, rights = [], []
                for i in range(SUB):
                    code = lists_s[t, first + i]
                    a = pl.multiple_of((code >> 8) * KS, KS)
                    b = pl.multiple_of((code & 255) * KS, KS)
                    lefts.append(sa[pl.ds(a, KS), :])
                    rights.append(sb[pl.ds(b, KS), :])
                turned = jnp.concatenate(lefts, axis=0).T
                high = turned.astype(jnp.bfloat16)
                turned = jnp.concatenate([high, (turned - high.astype(jnp.float32)).astype(jnp.bfloat16)], axis=0)
                sums.append(dot(turned, jnp.concatenate(rights, axis=0)))
            for u in range(WAYS):
                acc[targets[u]] += sums[u]
            return 0

        lax.fori_loop(0, (starts[TILES] + WAYS - 1) // WAYS, block, 0)
        return turn + 1, (most + CHUNK - 1) // CHUNK

    lax.while_loop(lambda s: s[0] < s[1], one_round, (jnp.int32(0), jnp.int32(1)))
    for t in range(TILES):
        total = (acc[t, 0:TB, 0:TB] + acc[t, 0:TB, TB:]) + (acc[t, TB:, 0:TB] + acc[t, TB:, TB:])
        for half in range(2):
            out_ref[2 * t + half] = total[half * TB // 2 : (half + 1) * TB // 2, :]


VMEM = pl.BlockSpec(memory_space=pltpu.VMEM)
SMEM = pl.BlockSpec(memory_space=pltpu.SMEM)
PARAMS = pltpu.CompilerParams(vmem_limit_bytes=48 * 1024 * 1024)


def shift(block, by):
    return lax.ppermute(block, "x", [(i, (i + by) % 4) for i in range(4)])


def across(block):
    return lax.ppermute(block, "core", [(0, 1), (1, 0)])


def swap(block, axis):
    return lax.all_to_all(block, axis, split_axis=0, concat_axis=0, tiled=True)


def local(amplitudes, integrals, residual_in, task_lists, task_counts, amp_wanted, int_wanted, res_targets):
    f32 = jnp.float32
    lists = jnp.broadcast_to(task_lists.transpose(0, 3, 1, 2).reshape(1, 3, TB), (MEMBERS, 3, TB))
    lists = swap(lists, "grp")
    tiles = pl.pallas_call(
        turn_kernel,
        out_shape=pltpu.VMEM((T_AT, TB), f32),
        in_specs=[VMEM] * 2,
        out_specs=VMEM,
        scratch_shapes=[pltpu.VMEM((TILES, TB, TB), f32)],
    )(amplitudes, integrals)
    payload = pl.pallas_call(
        payload_kernel,
        out_shape=pltpu.VMEM((8, ROWS, TB), f32),
        in_specs=[SMEM] + [VMEM] * 5,
        out_specs=VMEM,
        scratch_shapes=[pltpu.VMEM((MEMBERS, 3, TB), f32)],
    )(task_counts, pltpu.with_memory_space_constraint(tiles, pltpu.VMEM), pltpu.with_memory_space_constraint(lists, pltpu.VMEM), amp_wanted, int_wanted, res_targets)
    here = swap(payload, "z")
    left, right, here_far = shift(here, 1), shift(here, -1), across(here)
    ahead, behind, here_far = lax.optimization_barrier((shift(left[:4], 1), shift(right[4:], -1), here_far))
    opposite = jnp.concatenate([ahead, behind])
    near = [here, left, right, opposite]
    far = [here_far, across(left), across(right), across(opposite)]
    bf16 = jnp.bfloat16
    partial = pl.pallas_call(
        ladder_kernel,
        out_shape=pltpu.VMEM((MEMBERS, TB // 2, TB), f32),
        in_specs=[VMEM] * 8,
        out_specs=VMEM,
        scratch_shapes=[
            pltpu.VMEM(((ALL_TILES + 1) * KS, TB), f32),
            pltpu.VMEM((ALL_TILES * KS, 2 * TB), bf16),
            pltpu.VMEM((TILES, 2 * TB, 2 * TB), f32),
            pltpu.VMEM((LISTS, TB), f32),
            pltpu.VMEM((2, LISTS, TB), f32),
            pltpu.VMEM((LISTS, (2 + TILES) * TB), bf16),
            pltpu.VMEM((2 * TILES, WIDTH), jnp.int32),
            pltpu.SMEM((2 * TILES, WIDTH), jnp.int32),
            pltpu.SemaphoreType.DMA,
        ],
        compiler_params=PARAMS,
    )(*near, *far)
    halves = residual_in.reshape(MEMBERS, TB // 2, TB)
    half = lax.dynamic_index_in_dim(halves, lax.axis_index("grp"), 0, keepdims=False)
    half = half + jnp.sum(swap(partial, "grp"), axis=0)
    whole = swap(jnp.broadcast_to(half[None], halves.shape), "grp")
    return whole.reshape(TILES, TB, TB)


def solution(mesh):
    fine = Mesh(mesh.devices.reshape(8, 4, 2, MEMBERS), ("z", "x", "core", "grp"))
    wide = ("z", "x", "core")
    placed = (
        P(wide, None, None),
        P(wide, None, None),
        P(wide, None, None),
        P(wide, "grp", None, None),
        P(wide, None),
        P(wide, None),
        P(wide, None),
        P(wide, None),
    )
    return jax.shard_map(local, mesh=fine, in_specs=placed, out_specs=P(wide, None, None), check_vma=False)
```

```python
import jax
import jax.numpy as jnp
from jax import lax
from jax.experimental import pallas as pl
from jax.experimental.pallas import tpu as pltpu
from jax.sharding import Mesh, PartitionSpec as P

TB = 128
TILES = 4
OWNERS = 64
MEMBERS = 8
KS = TB // MEMBERS
ALL_TILES = OWNERS * TILES
ROWS = 2 * TILES * KS + 16
LIST_ROWS = 5
A_AT, B_AT, T_AT = 0, TILES * KS, 2 * TILES * KS
LISTS = OWNERS * LIST_ROWS
CHUNK = 288
SUB = 32
WAYS = 3
WIDTH = CHUNK + 96

NT = (((1,), (1,)), ((), ()))
TN = (((0,), (0,)), ((), ()))


def dot(a, b, dims=(((1,), (0,)), ((), ()))):
    return lax.dot_general(a, b, dims, preferred_element_type=jnp.float32)


def turn_kernel(amp_ref, int_ref, out_ref, turned):
    first = pl.multiple_of(lax.axis_index("grp") * KS, KS)
    for at, tiles in ((A_AT, amp_ref), (B_AT, int_ref)):
        for t in range(TILES):
            turned[t] = tiles[t].T
        for t in range(TILES):
            out_ref[at + t * KS : at + (t + 1) * KS, :] = turned[t, pl.ds(first, KS), :]


def payload_kernel(counts_ref, tiles_ref, lists_ref, amp_ref, int_ref, res_ref, out_ref, joined):
    owner = lax.broadcasted_iota(jnp.int32, (OWNERS, MEMBERS * TB), 0)
    slot = lax.broadcasted_iota(jnp.int32, (OWNERS, TB), 1)
    live = jnp.concatenate([(slot < counts_ref[0, m]).astype(jnp.float32) for m in range(MEMBERS)], axis=1)
    number = lax.broadcasted_iota(jnp.int32, (8, OWNERS), 1) * TILES
    kinds = []
    for kind, table in enumerate((amp_ref, int_ref, res_ref)):
        hit = jnp.concatenate([lists_ref[m, kind : kind + 1, :] for m in range(MEMBERS)], axis=1) == owner
        hit = jnp.where(hit, live if kind == 2 else 1.0, 0.0)
        names = number + table[0:1, :] + (1 if kind == 2 else 0)
        row = dot(names.astype(jnp.bfloat16), hit.astype(jnp.bfloat16))[0:1]
        kinds.append(row - 1.0 if kind == 2 else row)
    kinds = jnp.concatenate(kinds, axis=0)
    lists = [kinds[:, m * TB : (m + 1) * TB] for m in range(MEMBERS)]
    joined[...] = jnp.full_like(joined, -1.0)
    lane = lax.broadcasted_iota(jnp.int32, (3, TB), 1)
    at = jnp.int32(0)
    for m in range(MEMBERS):
        row, by = at // TB, at % TB
        turned = pltpu.roll(lists[m], by, 1)
        joined[row] = jnp.where(lane >= by, turned, joined[row])
        joined[row + 1] = jnp.where(lane < by, turned, joined[row + 1])
        at = at + counts_ref[0, m]
    rows = [joined[i, kind : kind + 1, :] for kind in range(3) for i in range(LIST_ROWS)]
    rows = jnp.concatenate(rows + [jnp.zeros((1, TB), jnp.float32)], axis=0)
    for z in range(8):
        out_ref[z, 0:T_AT, :] = tiles_ref[...]
        out_ref[z, T_AT:ROWS, :] = rows


def ladder_kernel(*refs):
    blocks, (out_ref, sa, sb, acc, wanted, plain, names, lists_v, lists_s, sem) = refs[:8], refs[8:]
    me = ((lax.axis_index("z") * 4) + lax.axis_index("x")) * 2 + lax.axis_index("core")
    core = lax.axis_index("core")
    my_x = lax.axis_index("x")

    at = 0
    for ref in blocks:
        for z in range(8):
            for kind, table in enumerate((plain.at[0], plain.at[1], wanted)):
                rows = ref[z, T_AT + kind * LIST_ROWS : T_AT + (kind + 1) * LIST_ROWS, :]
                table[at : at + LIST_ROWS, :] = rows
            at += LIST_ROWS
    for kind in range(2):
        names[:, kind * TB : (kind + 1) * TB] = plain[kind].astype(jnp.bfloat16)

    upto = lax.broadcasted_iota(jnp.int32, (TB, TB), 0) <= lax.broadcasted_iota(jnp.int32, (TB, TB), 1)
    upto = upto.astype(jnp.bfloat16)
    ones = jnp.ones((8, TB), jnp.bfloat16)

    def pick(base):
        hits = []
        for t in range(TILES):
            hit = wanted[...] == (me * TILES + t).astype(jnp.float32)
            hits.append(hit.astype(jnp.float32).astype(jnp.bfloat16))
        totals = [dot(ones, hit, NT) for hit in hits]
        for t in range(TILES):
            place = dot(hits[t], upto)
            names[:, (2 + t) * TB : (3 + t) * TB] = place.astype(jnp.bfloat16) * hits[t]
        lowers, uppers, sums = [], [], []
        for t in range(TILES):
            carry = jnp.zeros((8, 1), jnp.float32)
            upper = []
            for i in range(0, LISTS, TB):
                piece = totals[t][:, i : i + TB].astype(jnp.bfloat16)
                within = dot(piece, upto[: piece.shape[1], : piece.shape[1]])
                upper.append(within + carry)
                carry = carry + within[:, -1:]
            uppers.append(jnp.concatenate(upper, axis=1))
            lowers.append(uppers[t] - totals[t])
            sums.append(carry)
        rank = (base + lax.broadcasted_iota(jnp.int32, (CHUNK, LISTS), 0)).astype(jnp.float32)
        entry = (base + lax.broadcasted_iota(jnp.int32, (8, CHUNK), 1)).astype(jnp.float32)
        rows = [(lowers[t][0:1] <= rank) & (rank < uppers[t][0:1]) for t in range(TILES)]
        before = [jnp.sum(jnp.where(rows[t], lowers[t][0:1], 0.0), axis=1, keepdims=True) for t in range(TILES)]
        rows = [row.astype(jnp.float32).astype(jnp.bfloat16) for row in rows]
        found = [dot(rows[t], names[:, 0 : 2 * TB]) for t in range(TILES)]
        places = [dot(rows[t], names[:, (2 + t) * TB : (3 + t) * TB]) for t in range(TILES)]
        for t in range(TILES):
            chosen = places[t] == rank[:, 0:1] + 1.0 - before[t]
            left = dot(ones, jnp.where(chosen, found[t][:, 0:TB], 0.0).astype(jnp.bfloat16), NT)
            right = dot(ones, jnp.where(chosen, found[t][:, TB : 2 * TB], 0.0).astype(jnp.bfloat16), NT)
            code = jnp.where(entry < sums[t], left * 256.0 + right, float(ALL_TILES * 256))
            lists_v[t : t + 1, 0:CHUNK] = code[0:1].astype(jnp.int32)
            lists_v[t : t + 1, CHUNK:] = jnp.full((1, WIDTH - CHUNK), ALL_TILES * 256, jnp.int32)
            lists_v[TILES + t : TILES + t + 1, :] = jnp.broadcast_to(sums[t][0:1], (1, WIDTH)).astype(jnp.int32)

    def spread(z):
        for i, ref in enumerate(blocks):
            c = core if i < 4 else 1 - core
            owner = (z * 4 + (my_x + (0, 3, 1, 2)[i % 4]) % 4) * 2 + c
            to = pl.ds(pl.multiple_of(owner * TILES * KS, TILES * KS), TILES * KS)
            for at, store in ((A_AT, sa), (B_AT, sb)):
                value = ref[z, at : at + TILES * KS, :]
                if store is sa:
                    store[to, :] = value
                    continue
                high = value.astype(jnp.bfloat16)
                store[to, 0:TB] = high
                store[to, TB : 2 * TB] = (value - high.astype(jnp.float32)).astype(jnp.bfloat16)

    def one_round(state):
        turn, _ = state
        base = turn * CHUNK
        pick(base)
        copy = pltpu.make_async_copy(lists_v, lists_s, sem)
        copy.start()

        @pl.when(turn == 0)
        def _():
            for z in range(8):
                spread(z)
            sa[ALL_TILES * KS :, :] = jnp.zeros((KS, TB), jnp.float32)
            acc[...] = jnp.zeros_like(acc)

        copy.wait()
        most, starts = jnp.int32(0), [jnp.int32(0)]
        for t in range(TILES):
            total = lists_s[TILES + t, 0]
            most = jnp.maximum(most, total)
            starts.append(starts[t] + (jnp.clip(total - base, 0, CHUNK) + SUB - 1) // SUB)

        def block(index, _):
            targets, sums = [], []
            for u in range(WAYS):
                at = index * WAYS + u
                t = (at >= starts[1]).astype(jnp.int32) + (at >= starts[2]).astype(jnp.int32) + (at >= starts[3]).astype(jnp.int32)
                first = jnp.where(t == 0, 0, jnp.where(t == 1, starts[1], jnp.where(t == 2, starts[2], starts[3])))
                first = (at - first) * SUB
                targets.append(t)
                lefts, rights = [], []
                for i in range(SUB):
                    code = lists_s[t, first + i]
                    a = pl.multiple_of((code >> 8) * KS, KS)
                    b = pl.multiple_of((code & 255) * KS, KS)
                    lefts.append(sa[pl.ds(a, KS), :])
                    rights.append(sb[pl.ds(b, KS), :])
                turned = jnp.concatenate(lefts, axis=0).T
                high = turned.astype(jnp.bfloat16)
                turned = jnp.concatenate([high, (turned - high.astype(jnp.float32)).astype(jnp.bfloat16)], axis=0)
                sums.append(dot(turned, jnp.concatenate(rights, axis=0)))
            for u in range(WAYS):
                acc[targets[u]] += sums[u]
            return 0

        lax.fori_loop(0, (starts[TILES] + WAYS - 1) // WAYS, block, 0)
        return turn + 1, (most + CHUNK - 1) // CHUNK

    lax.while_loop(lambda s: s[0] < s[1], one_round, (jnp.int32(0), jnp.int32(1)))
    for t in range(TILES):
        total = (acc[t, 0:TB, 0:TB] + acc[t, 0:TB, TB:]) + (acc[t, TB:, 0:TB] + acc[t, TB:, TB:])
        for half in range(2):
            out_ref[2 * t + half] = total[half * TB // 2 : (half + 1) * TB // 2, :]


VMEM = pl.BlockSpec(memory_space=pltpu.VMEM)
SMEM = pl.BlockSpec(memory_space=pltpu.SMEM)
PARAMS = pltpu.CompilerParams(vmem_limit_bytes=48 * 1024 * 1024)


def shift(block, by):
    return lax.ppermute(block, "x", [(i, (i + by) % 4) for i in range(4)])


def across(block):
    return lax.ppermute(block, "core", [(0, 1), (1, 0)])


def swap(block, axis):
    return lax.all_to_all(block, axis, split_axis=0, concat_axis=0, tiled=True)


def local(amplitudes, integrals, residual_in, task_lists, task_counts, amp_wanted, int_wanted, res_targets):
    f32 = jnp.float32
    lists = jnp.broadcast_to(task_lists.transpose(0, 3, 1, 2).reshape(1, 3, TB), (MEMBERS, 3, TB))
    lists = swap(lists, "grp")
    tiles = pl.pallas_call(
        turn_kernel,
        out_shape=pltpu.VMEM((T_AT, TB), f32),
        in_specs=[VMEM] * 2,
        out_specs=VMEM,
        scratch_shapes=[pltpu.VMEM((TILES, TB, TB), f32)],
    )(amplitudes, integrals)
    payload = pl.pallas_call(
        payload_kernel,
        out_shape=pltpu.VMEM((8, ROWS, TB), f32),
        in_specs=[SMEM] + [VMEM] * 5,
        out_specs=VMEM,
        scratch_shapes=[pltpu.VMEM((MEMBERS, 3, TB), f32)],
    )(task_counts, pltpu.with_memory_space_constraint(tiles, pltpu.VMEM), pltpu.with_memory_space_constraint(lists, pltpu.VMEM), amp_wanted, int_wanted, res_targets)
    here = swap(payload, "z")
    left, right, here_far = shift(here, 1), shift(here, -1), across(here)
    ahead, behind, here_far = lax.optimization_barrier((shift(left[:4], 1), shift(right[4:], -1), here_far))
    opposite = jnp.concatenate([ahead, behind])
    near = [here, left, right, opposite]
    far = [here_far, across(left), across(right), across(opposite)]
    bf16 = jnp.bfloat16
    partial = pl.pallas_call(
        ladder_kernel,
        out_shape=pltpu.VMEM((MEMBERS, TB // 2, TB), f32),
        in_specs=[VMEM] * 8,
        out_specs=VMEM,
        scratch_shapes=[
            pltpu.VMEM(((ALL_TILES + 1) * KS, TB), f32),
            pltpu.VMEM((ALL_TILES * KS, 2 * TB), bf16),
            pltpu.VMEM((TILES, 2 * TB, 2 * TB), f32),
            pltpu.VMEM((LISTS, TB), f32),
            pltpu.VMEM((2, LISTS, TB), f32),
            pltpu.VMEM((LISTS, (2 + TILES) * TB), bf16),
            pltpu.VMEM((2 * TILES, WIDTH), jnp.int32),
            pltpu.SMEM((2 * TILES, WIDTH), jnp.int32),
            pltpu.SemaphoreType.DMA,
        ],
        compiler_params=PARAMS,
    )(*near, *far)
    halves = residual_in.reshape(MEMBERS, TB // 2, TB)
    half = lax.dynamic_index_in_dim(halves, lax.axis_index("grp"), 0, keepdims=False)
    half = half + jnp.sum(swap(partial, "grp"), axis=0)
    whole = swap(jnp.broadcast_to(half[None], halves.shape), "grp")
    return whole.reshape(TILES, TB, TB)


def solution(mesh):
    fine = Mesh(mesh.devices.reshape(8, 4, 2, MEMBERS), ("z", "x", "core", "grp"))
    wide = ("z", "x", "core")
    placed = (
        P(wide, None, None),
        P(wide, None, None),
        P(wide, None, None),
        P(wide, "grp", None, None),
        P(wide, None),
        P(wide, None),
        P(wide, None),
        P(wide, None),
    )
    return jax.shard_map(local, mesh=fine, in_specs=placed, out_specs=P(wide, None, None), check_vma=False)
```
